32 devices in a mesh: grp: 2 (over y), leaf: 4 (over z), limb: 2 (over x), coef: 2 (over core).
Axes of the slice: x: 2, y: 2, z: 4, core: 2. Of those that a mesh axis runs over, the one named last changes fastest.
Arguments:
- root_keys: bfloat16 [8, 1, 2, 12, 256, 128], P(('grp', 'leaf'), None, None, 'limb', 'coef'), parts along dimension 0, may hold values from -6 to 6
- switch_main: bfloat16 [8, 2, 4, 2, 12, 256, 128], P(('grp', 'leaf'), None, None, None, 'limb', 'coef'), parts along dimension 0, may hold values from -3 to 3
- switch_special: bfloat16 [8, 2, 4, 2, 4, 256, 128], P(('grp', 'leaf'), None, None, None, 'limb', 'coef'), parts along dimension 0, may hold values from -3 to 3
- basis_up: bfloat16 [4, 16, 3], replicated, may hold values from -3.5 to 3.5
- basis_down: bfloat16 [12, 4], P('limb'), may hold values from -3 to 3
- special_inverse: float32 [12], P('limb'), may hold values from 0.5 to 2
- parent_table: int32 [2, 8], P(None, 'grp'), parts along dimension 1, may hold values from 0 to 3, as said below
- owner_table: int32 [8], P('grp'), parts along dimension 0, may hold values from 0 to 3, as said below
Outputs:
- delivered: bfloat16 [8, 3, 1, 2, 12, 256, 128], P(('grp', 'leaf'), None, None, None, 'limb', 'coef'), parts along dimension 0
The draws below stay inside these ranges and needn't reach their ends.
There are 2 independent parts, one for each index of `grp`. The reference program is written for one: setup_inputs(seed, part) draws one part's arguments, and reference() takes and returns one part's arrays. A program takes and returns all parts, laid end to end along the dimension named above; an argument that names none is the same for every part. Nothing has to cross between parts.
Inputs may be any that keep to these rules, and one draw needn't show every extreme that they name: parent_table[l, j] = (j + e) mod 4 with e from -2 to 2; in every row e = 2 for some j and e = -2 for another j. `owner_table`: each value is taken by at most 3 entries, and by exactly 3 entries for some value.
All inputs are finite; a program needn't handle non-finite values.
Results may differ from the reference program's by a relative error of at most 0.025.
Values may be sent and summed in bfloat16 or wider, within the bound.
A program may use at most 64 MiB of HBM per device.

```python
import math
import jax
import jax.numpy as jnp
from jax import lax

N1 = 128
N2 = 256
LQ = 12
LP = 4
DIGITS = 4
DLIMBS = 3
COMPS = 1
LEVELS = 2
RADIUS = 2
CAP = 3
LEAVES = 4


def draw_parent_table(key, part):
    parent_rows = []
    for tree_level in range(LEVELS):
        level_key = jax.random.fold_in(key, 101 + tree_level)
        offsets = jax.random.randint(jax.random.fold_in(level_key, 1), (LEAVES,), -RADIUS, RADIUS + 1)
        shuffled = jax.random.permutation(jax.random.fold_in(level_key, 2), LEAVES)
        offsets = offsets.at[shuffled[0]].set(RADIUS).at[shuffled[1]].set(-RADIUS)
        parent_rows.append((jnp.arange(LEAVES) + offsets) % LEAVES)
    return jnp.stack(parent_rows).astype(jnp.int32)


def draw_owner_table(key, part):
    slot_count = LEAVES * CAP
    shuffled = jax.random.permutation(jax.random.fold_in(key, 7), slot_count)
    favoured = shuffled[0] // CAP
    ranking = jnp.argsort(shuffled)
    slot_ids = jnp.arange(slot_count)
    priority = jnp.where(slot_ids // CAP == favoured, -1, ranking)
    chosen = jnp.argsort(priority, stable=True)[:LEAVES]
    owners = chosen // CAP
    mixing = jax.random.permutation(jax.random.fold_in(key, 8), LEAVES)
    return owners[mixing].astype(jnp.int32)


def shard_levels(own_key, dims, shards, low, high):
    def one(axis_at, blocks):
        draws = jax.random.uniform(jax.random.fold_in(jax.random.fold_in(own_key, 6), axis_at), (blocks,), jnp.float32, low / len(shards), high / len(shards))
        return jnp.repeat(jnp.exp(draws), dims[axis_at] // blocks).reshape((-1,) + (1,) * (len(dims) - axis_at - 1))

    factor_of = one(*shards[0])
    for cut in shards[1:]:
        factor_of = factor_of * one(*cut)
    return factor_of


def scatter_about(stream_key, extent, width, bound, pieces=(), kind=jnp.bfloat16):
    values = jax.random.normal(stream_key, extent, jnp.float32) * width
    if len(pieces) > 0:
        values = shard_levels(stream_key, extent, pieces, -0.22, 0.18) * values
    return jnp.clip(values, min=-bound, max=bound).astype(kind)


def setup_inputs(seed: int = 0, part: int = 0) -> dict:
    keys = jax.random.split(jax.random.key(seed), 9)
    own_keys = jax.random.split(jax.random.fold_in(keys[8], part), 9)
    root_keys = scatter_about(own_keys[0], (LEAVES, COMPS, 2, LQ, N2, N1), 1.0, 6.0, ((0, 4), (3, 2), (4, 2)))
    switch_main = scatter_about(own_keys[1], (LEAVES, LEVELS, DIGITS, 2, LQ, N2, N1), DIGITS ** -0.5, 3.0, ((0, 4), (4, 2), (5, 2)))
    switch_special = scatter_about(own_keys[2], (LEAVES, LEVELS, DIGITS, 2, LP, N2, N1), DIGITS ** -0.5, 3.0, ((0, 4), (4, 2), (5, 2)))
    basis_up = scatter_about(keys[3], (DIGITS, LQ + LP, DLIMBS), DLIMBS ** -0.5, 3.5)
    basis_down = scatter_about(keys[4], (LQ, LP), LP ** -0.5, 3.0, ((0, 2),))
    special_inverse = jnp.clip(jnp.exp(math.log(2.0) - 1.3862944 * jax.random.uniform(keys[5], (LQ,), jnp.float32) ** shard_levels(keys[5], (LQ,), ((0, 2),), -0.2, 0.2)), 0.5, 2.0)
    parent_table = draw_parent_table(jax.random.fold_in(jax.random.fold_in(keys[8], part), 71), part)
    owner_table = draw_owner_table(jax.random.fold_in(jax.random.fold_in(keys[8], part), 71), part)
    return {"root_keys": root_keys, "switch_main": switch_main, "switch_special": switch_special, "basis_up": basis_up, "basis_down": basis_down, "special_inverse": special_inverse, "parent_table": parent_table, "owner_table": owner_table}


def cosine_table(length):
    frequency = jnp.arange(length).astype(jnp.float32)[:, None]
    sample = jnp.arange(length).astype(jnp.float32)[None, :]
    weight = jnp.where(frequency == 0, jnp.sqrt(1.0 / length), jnp.sqrt(2.0 / length))
    return (weight * jnp.cos(math.pi * (2.0 * sample + 1.0) * frequency / (2.0 * length))).astype(jnp.bfloat16)

def limb_twist(limb_ids):
    multiplier = 2 * limb_ids + 1
    product = multiplier[:, None, None] * jnp.arange(N1)[None, :, None] * jnp.arange(N2)[None, None, :] % N2
    return 1.0 + 0.5 * jnp.cos(2.0 * math.pi * product.astype(jnp.float32) / N2)

def forward(values, tables, twisting):
    short_cosine, long_cosine = tables
    halfway = jnp.einsum('...ab,kb->...ka', values.astype(jnp.float32), long_cosine.astype(jnp.float32))
    halfway = (halfway * jnp.swapaxes(twisting, -1, -2)).astype(jnp.bfloat16)
    return jnp.einsum('...kn,jn->...kj', halfway.astype(jnp.float32), short_cosine.astype(jnp.float32))

def inverse(values, tables, twisting):
    short_cosine, long_cosine = tables
    halfway = jnp.einsum('...kj,jn->...nk', values.astype(jnp.float32), short_cosine.astype(jnp.float32))
    halfway = (halfway / twisting).astype(jnp.bfloat16)
    return jnp.einsum('...nk,kb->...nb', halfway.astype(jnp.float32), long_cosine.astype(jnp.float32))

def derive(parent_key, main_key, special_key, basis_up, basis_down, special_inverse, tables, twist_all):
    twist_main = twist_all[:LQ]
    twist_special = twist_all[LQ:]
    digits = inverse(parent_key[:, 1], tables, twist_main).astype(jnp.bfloat16)
    digits = digits.reshape(COMPS, DIGITS, LQ // DIGITS, N1, N2)
    raised = jnp.einsum('cdsab,dts->cdtab', digits.astype(jnp.float32), basis_up.astype(jnp.float32)).astype(jnp.bfloat16)
    raised_hat = forward(raised, tables, twist_all)
    switch_all = jnp.concatenate([main_key, special_key], axis=2).astype(jnp.float32)
    summed = jnp.einsum('cdtkj,dqtkj->cqtkj', raised_hat, switch_all)
    upper_part = summed[:, :, LQ:].astype(jnp.bfloat16)
    lowered = inverse(upper_part, tables, twist_special).astype(jnp.bfloat16)
    converted = jnp.einsum('cqpab,lp->cqlab', lowered.astype(jnp.float32), basis_down.astype(jnp.float32)).astype(jnp.bfloat16)
    correction = forward(converted, tables, twist_main)
    result = (summed[:, :, :LQ] - correction) * special_inverse[None, None, :, None, None]
    leading = parent_key[:, 0].astype(jnp.float32) + result[:, 0]
    return jnp.stack([leading, result[:, 1]], axis=1).astype(jnp.bfloat16)

def reference(root_keys, switch_main, switch_special, basis_up, basis_down, special_inverse, parent_table, owner_table):
    tables = (cosine_table(N1), cosine_table(N2))
    twist_all = limb_twist(jnp.arange(LQ + LP))
    current = root_keys
    for tree_level in range(LEVELS):
        parents = jnp.take(current, parent_table[tree_level], axis=0)

        def derive_one(packed):
            return derive(packed[0], packed[1], packed[2], basis_up, basis_down, special_inverse, tables, twist_all)
        current = lax.map(derive_one, (parents, switch_main[:, tree_level], switch_special[:, tree_level]))
    position = jnp.arange(LEAVES)
    same_owner = owner_table[:, None] == owner_table[None, :]
    rank_within = lax.optimization_barrier(jnp.sum((same_owner & (position[:, None] < position[None, :])).astype(jnp.int32), axis=0))
    slot_ids = jnp.arange(LEAVES * CAP)
    matches = (owner_table[None, :] == (slot_ids // CAP)[:, None]) & (rank_within[None, :] == (slot_ids % CAP)[:, None])
    source = lax.optimization_barrier(jnp.sum(jnp.where(matches, position[None, :], 0), axis=1)).astype(jnp.int32)
    filled = jnp.any(matches, axis=1)
    gathered = jnp.take(current, source, axis=0)
    gathered = jnp.where(filled[:, None, None, None, None, None], gathered, jnp.zeros((), gathered.dtype))
    return gathered.reshape((LEAVES, CAP) + current.shape[1:])
```

```python
import functools
import math

import jax
import jax.numpy as jnp
import ml_dtypes
import numpy as np
from jax import lax
from jax.experimental import pallas as pl
from jax.experimental.pallas import tpu as pltpu
from jax.sharding import PartitionSpec as P

MESH = pl.DeviceIdType.MESH
CHUNK = 3


def cosine_table(length):
    frequency = np.arange(length).astype(np.float32)[:, None]
    sample = np.arange(length).astype(np.float32)[None, :]
    weight = np.where(
        frequency == 0, np.sqrt(np.float32(1.0 / length)), np.sqrt(np.float32(2.0 / length))
    )
    angle = np.float32(math.pi) * (np.float32(2.0) * sample + np.float32(1.0)) * frequency
    angle = angle / np.float32(2.0 * length)
    return (weight * np.cos(angle)).astype(ml_dtypes.bfloat16)


def twist_table(limbs, n1, n2):
    product = (
        (2 * np.arange(limbs) + 1)[:, None, None]
        * np.arange(n2)[None, :, None]
        * np.arange(n1)[None, None, :]
        % n2
    )
    return 1.0 + 0.5 * np.cos(2.0 * math.pi * product / n2)


def dot(a, b):
    return jnp.dot(a, b, preferred_element_type=jnp.float32)


def pick(n, index, load):
    if n <= 8:
        value = load(0)
        for j in range(1, n):
            value = jnp.where(index == j, load(j), value)
        return value
    return lax.fori_loop(
        1, n, lambda j, value: jnp.where(index == j, load(j), value), load(0)
    )


def repeat(low, high, body):
    if high - low <= 3:
        for i in range(low, high):
            body(i)
    else:
        lax.fori_loop(low, high, lambda i, c: (body(i), c)[1], 0)


def kernel(
    cfg,
    parent_ref,
    owner_ref,
    up_ref,
    down_ref,
    inv_ref,
    c1_ref,
    c1t_ref,
    d_ref,
    root_ref,
    main_hbm,
    special_hbm,
    twist_hbm,
    recip_hbm,
    out_ref,
    main_key,
    special_key,
    twist,
    recip,
    z_buf,
    x_gather,
    b_gather,
    f_gather,
    x_buf,
    z2_buf,
    x2_buf,
    s_main,
    s_special,
    b_add,
    load_sem,
    route_send,
    route_recv,
    z_sem,
    x_send,
    x_recv,
    z2_sem,
    x2_send,
    x2_recv,
):
    n, nl, lm, ls, lq, lp, digits, levels, cap, half = cfg
    width = CHUNK
    chunks = lm // width
    me = lax.axis_index("leaf")
    limb = lax.axis_index("limb")
    coef = lax.axis_index("coef")
    other = 1 - coef

    loads = []
    for l in range(levels):
        loads.append(pltpu.make_async_copy(main_hbm.at[0, l], main_key.at[l], load_sem.at[l]))
        loads.append(
            pltpu.make_async_copy(special_hbm.at[0, l], special_key.at[l], load_sem.at[levels + l])
        )
    rows = pl.ds(pl.multiple_of(coef * half, half), half)
    tables = []
    for k, (src, dst) in enumerate(((recip_hbm, recip), (twist_hbm, twist))):
        tables.append(
            pltpu.make_async_copy(
                src.at[pl.ds(limb * lm, lm), rows], dst.at[pl.ds(0, lm)], load_sem.at[2 * levels + 2 * k]
            )
        )
        tables.append(
            pltpu.make_async_copy(
                src.at[pl.ds(lq + limb * ls, ls), rows],
                dst.at[pl.ds(lm, ls)],
                load_sem.at[2 * levels + 2 * k + 1],
            )
        )
    for copy in tables + loads:
        copy.start()

    barrier = pltpu.get_barrier_semaphore()

    @pl.when(me > 0)
    def _():
        pl.semaphore_signal(barrier, inc=1, device_id={"leaf": me - 1}, device_id_type=MESH)

    @pl.when(me < n - 1)
    def _():
        pl.semaphore_signal(barrier, inc=1, device_id={"leaf": me + 1}, device_id_type=MESH)

    pl.semaphore_signal(barrier, inc=1, device_id={"coef": other}, device_id_type=MESH)
    for k in range(1, nl):
        pl.semaphore_signal(
            barrier, inc=1, device_id={"limb": lax.rem(limb + k, nl)}, device_id_type=MESH
        )
    neighbours = jnp.where(me > 0, 1, 0) + jnp.where(me < n - 1, 1, 0)
    pl.semaphore_wait(barrier, nl + neighbours)

    def hop(unit, piece, slot, c, way):
        target = me + 1 if way == 0 else me - 1
        return pltpu.make_async_remote_copy(
            src_ref=piece(slot, c),
            dst_ref=piece(slot, c),
            send_sem=route_send.at[unit, way, slot, c],
            recv_sem=route_recv.at[unit, slot, c],
            device_id={"leaf": target},
            device_id_type=MESH,
        )

    def route_start(unit, piece, c):
        @pl.when(me < n - 1)
        def _():
            hop(unit, piece, me, c, 0).start()

        @pl.when(me > 0)
        def _():
            hop(unit, piece, me, c, 1).start()

    def route_step(unit, piece, s, c):
        @pl.when(me >= s)
        def _():
            hop(unit, piece, me - s, c, 0).wait_recv()

            @pl.when(me < n - 1)
            def _():
                hop(unit, piece, me - s, c, 0).start()

        @pl.when(me + s <= n - 1)
        def _():
            hop(unit, piece, me + s, c, 1).wait_recv()

            @pl.when(me > 0)
            def _():
                hop(unit, piece, me + s, c, 1).start()

    def route_steps(unit, piece, low, high):
        def one(s):
            for c in range(chunks):
                route_step(unit, piece, s, c)

        repeat(low, high, one)

    def route_end(unit, piece):
        def one(slot):
            for c in range(chunks):

                @pl.when((slot <= me) & (me < n - 1))
                def _():
                    hop(unit, piece, slot, c, 0).wait_send()

                @pl.when((slot >= me) & (me > 0))
                def _():
                    hop(unit, piece, slot, c, 1).wait_send()

        repeat(0, n, one)

    def part(c):
        return pl.ds(c * width, width)

    def piece_of(buf, *lead):
        return lambda slot, c: buf.at[(*lead, slot, part(c))]

    c1 = c1_ref[...]
    c1t = c1t_ref[...]
    d_own = d_ref[rows, :]

    def z_copy(buf, sem, l, c, where):
        return pltpu.make_async_remote_copy(
            src_ref=buf.at[l, coef, where],
            dst_ref=buf.at[l, coef, where],
            send_sem=sem.at[l, 0, c],
            recv_sem=sem.at[l, 1, c],
            device_id={"coef": other},
            device_id_type=MESH,
        )

    def mixed(buf, l, t):
        own = buf[l, coef, t].astype(jnp.float32)
        return own + dot(d_own[:, :half], buf[l, 0, t]) + dot(d_own[:, half:], buf[l, 1, t])

    def x_copy(l, c, k):
        return pltpu.make_async_remote_copy(
            src_ref=x_buf.at[l, limb, part(c)],
            dst_ref=x_buf.at[l, limb, part(c)],
            send_sem=x_send.at[l, c, k - 1],
            recv_sem=x_recv.at[l, c, k - 1],
            device_id={"limb": lax.rem(limb + k, nl)},
            device_id_type=MESH,
        )

    def x2_copy(l, k):
        return pltpu.make_async_remote_copy(
            src_ref=x2_buf.at[l, limb],
            dst_ref=x2_buf.at[l, limb],
            send_sem=x2_send.at[l, k - 1],
            recv_sem=x2_recv.at[l, k - 1],
            device_id={"limb": lax.rem(limb + k, nl)},
            device_id_type=MESH,
        )

    def switched(l, t_global, t_twist, key_of):
        sums = [None, None]
        w = twist[t_twist]
        for d in range(digits):
            total = None
            for s in range(CHUNK):
                at = d * CHUNK + s
                term = x_buf[l, at // lm, at % lm].astype(jnp.float32)
                term = term * up_ref[(d * (lq + lp) + t_global) * CHUNK + s]
                total = term if total is None else total + term
            hat = dot((total * w).astype(jnp.bfloat16), c1t)
            for i in range(2):
                add = hat * key_of(d, i).astype(jnp.float32)
                sums[i] = add if sums[i] is None else sums[i] + add
        return sums

    def corrected(l, i, q):
        total = None
        for p in range(lp):
            term = x2_buf[l, p // ls, i * ls + p % ls].astype(jnp.float32) * down_ref[q * lp + p]
            total = term if total is None else total + term
        hat = dot((total * twist[q]).astype(jnp.bfloat16), c1t)
        return (s_main[i, q] - hat) * inv_ref[q]

    b_gather[0, me] = root_ref[0]
    tables[0].wait()
    tables[1].wait()

    def send_z(l, t, value):
        z_buf[l, coef, t] = (dot(value, c1) * recip[t]).astype(jnp.bfloat16)

    for c in range(chunks):
        for t in range(c * width, (c + 1) * width):
            send_z(0, t, root_ref[1, t])
        z_copy(z_buf, z_sem, 0, c, part(c)).start()
    tables[2].wait()
    tables[3].wait()

    for l in range(levels):
        parent = parent_ref[l * n + me]
        xp = piece_of(x_gather, l)
        bp = piece_of(b_gather, l)
        ux, ub = 2 * l, 2 * l + 1
        for c in range(chunks):
            z_copy(z_buf, z_sem, l, c, part(c)).wait_recv()
            for t in range(c * width, (c + 1) * width):
                x_gather[l, me, t] = mixed(z_buf, l, t).astype(jnp.bfloat16)
            route_start(ux, xp, c)
        if l > 0:
            route_steps(ub - 2, piece_of(b_gather, l - 1), 2, n)
            before = parent_ref[(l - 1) * n + me]
            for t in range(lm):
                held = pick(n, before, lambda j: b_gather[l - 1, j, t]).astype(jnp.float32)
                b_gather[l, me, t] = (held + b_add[t]).astype(jnp.bfloat16)
        route_steps(ux, xp, 1, n - 1)
        for c in range(chunks):
            route_step(ux, xp, n - 1, c)
            for t in range(c * width, (c + 1) * width):
                x_buf[l, limb, t] = pick(n, parent, lambda j: x_gather[l, j, t])
            for k in range(1, nl):
                x_copy(l, c, k).start()
            route_start(ub, bp, c)
        loads[2 * l].wait()
        loads[2 * l + 1].wait()
        for c in range(chunks):
            for k in range(1, nl):
                x_copy(l, c, k).wait_recv()

        for p in range(ls):
            sums = switched(
                l, lq + limb * ls + p, lm + p, lambda d, i: special_key[l, d, i, p]
            )
            for i in range(2):
                z = dot(sums[i].astype(jnp.bfloat16), c1) * recip[lm + p]
                z2_buf[l, coef, i * ls + p] = z.astype(jnp.bfloat16)
        everything = pl.ds(0, 2 * ls)
        z_copy(z2_buf, z2_sem, l, 0, everything).start()
        z_copy(z2_buf, z2_sem, l, 0, everything).wait_recv()
        for e in range(2 * ls):
            x2_buf[l, limb, e] = mixed(z2_buf, l, e).astype(jnp.bfloat16)
        for k in range(1, nl):
            x2_copy(l, k).start()

        def main_target(t, carry):
            sums = switched(l, limb * lm + t, t, lambda d, i: main_key[l, d, i, t])
            s_main[0, t] = sums[0]
            s_main[1, t] = sums[1]
            return carry

        lax.fori_loop(0, lm, main_target, 0)
        for k in range(1, nl):
            x2_copy(l, k).wait_recv()

        last = l == levels - 1
        for c in range(chunks):
            for t in range(c * width, (c + 1) * width):
                value = corrected(l, 1, t).astype(jnp.bfloat16)
                if last:
                    f_gather[1, me, t] = value
                else:
                    send_z(l + 1, t, value)
            if last:
                route_start(2 * levels, piece_of(f_gather, 1), c)
            else:
                z_copy(z_buf, z_sem, l + 1, c, part(c)).start()
        route_steps(ub, bp, 1, 2)

        def b_part(t, carry):
            b_add[t] = corrected(l, 0, t)
            return carry

        lax.fori_loop(0, lm, b_part, 0)

    l = levels - 1
    route_steps(2 * l + 1, piece_of(b_gather, l), 2, n)
    before = parent_ref[l * n + me]
    fa, fb = piece_of(f_gather, 1), piece_of(f_gather, 0)
    for c in range(chunks):
        for t in range(c * width, (c + 1) * width):
            held = pick(n, before, lambda j: b_gather[l, j, t]).astype(jnp.float32)
            f_gather[0, me, t] = (held + b_add[t]).astype(jnp.bfloat16)
        route_start(2 * levels + 1, fb, c)

    def both(s):
        for c in range(chunks):
            route_step(2 * levels, fa, s, c)
        for c in range(chunks):
            route_step(2 * levels + 1, fb, s, c)

    repeat(1, n, both)

    def seek(j, state):
        count, sources, found = state
        mine = (owner_ref[j] == me).astype(jnp.int32)
        hits = [mine * (count == s).astype(jnp.int32) for s in range(cap)]
        sources = tuple(src + hit * j for src, hit in zip(sources, hits))
        found = tuple(f + hit for f, hit in zip(found, hits))
        return count + mine, sources, found

    zero = jnp.int32(0)
    _, sources, found = lax.fori_loop(0, n, seek, (zero, (zero,) * cap, (zero,) * cap))
    for s in range(cap):
        for i in range(2):
            value = f_gather[i, sources[s]]
            out_ref[s, i] = jnp.where(found[s] > 0, value, jnp.zeros_like(value))

    for l in range(levels):
        route_end(2 * l, piece_of(x_gather, l))
        route_end(2 * l + 1, piece_of(b_gather, l))
        for c in range(chunks):
            z_copy(z_buf, z_sem, l, c, part(c)).wait_send()
            for k in range(1, nl):
                x_copy(l, c, k).wait_send()
        z_copy(z2_buf, z2_sem, l, 0, pl.ds(0, 2 * ls)).wait_send()
        for k in range(1, nl):
            x2_copy(l, k).wait_send()
    route_end(2 * levels, fa)
    route_end(2 * levels + 1, fb)


def per_device(
    n,
    nl,
    nc,
    root_keys,
    switch_main,
    switch_special,
    basis_up,
    basis_down,
    special_inverse,
    parent_table,
    owner_table,
):
    cap = 3
    _, levels, digits, _, lm, half, n1 = switch_main.shape
    ls = switch_special.shape[4]
    lq, lp = lm * nl, ls * nl
    n2 = half * nc
    chunks = lm // CHUNK
    c1 = cosine_table(n1)
    c2 = cosine_table(n2).astype(np.float64)
    gram = (c2 @ c2.T - np.eye(n2)).astype(np.float32).astype(ml_dtypes.bfloat16)
    table = twist_table(lq + lp, n1, n2)
    cfg = (n, nl, lm, ls, lq, lp, digits, levels, cap, half)
    bf16, f32 = jnp.bfloat16, jnp.float32
    tile = (half, n1)
    smem = pl.BlockSpec(memory_space=pltpu.SMEM)
    vmem = pl.BlockSpec(memory_space=pltpu.VMEM)
    hbm = pl.BlockSpec(memory_space=pl.ANY)
    dma = pltpu.SemaphoreType.DMA
    units = 2 * levels + 2
    out = pl.pallas_call(
        functools.partial(kernel, cfg),
        out_shape=jax.ShapeDtypeStruct((cap, 2, lm) + tile, bf16),
        in_specs=[smem] * 5 + [vmem] * 4 + [hbm] * 4,
        out_specs=vmem,
        scratch_shapes=[
            pltpu.VMEM((levels, digits, 2, lm) + tile, bf16),
            pltpu.VMEM((levels, digits, 2, ls) + tile, bf16),
            pltpu.VMEM((lm + ls,) + tile, f32),
            pltpu.VMEM((lm + ls,) + tile, f32),
            pltpu.VMEM((levels, 2, lm) + tile, bf16),
            pltpu.VMEM((levels, n, lm) + tile, bf16),
            pltpu.VMEM((levels, n, lm) + tile, bf16),
            pltpu.VMEM((2, n, lm) + tile, bf16),
            pltpu.VMEM((levels, nl, lm) + tile, bf16),
            pltpu.VMEM((levels, 2, 2 * ls) + tile, bf16),
            pltpu.VMEM((levels, nl, 2 * ls) + tile, bf16),
            pltpu.VMEM((2, lm) + tile, f32),
            pltpu.VMEM((2, ls) + tile, f32),
            pltpu.VMEM((lm,) + tile, f32),
            dma((2 * levels + 4,)),
            dma((units, 2, n, chunks)),
            dma((units, n, chunks)),
            dma((levels, 2, chunks)),
            dma((levels, chunks, nl - 1)),
            dma((levels, chunks, nl - 1)),
            dma((levels, 2, 1)),
            dma((levels, nl - 1)),
            dma((levels, nl - 1)),
        ],
        compiler_params=pltpu.CompilerParams(
            collective_id=0, has_side_effects=True, vmem_limit_bytes=56 * 1024 * 1024
        ),
        name="derive_and_deliver",
    )(
        parent_table.reshape(-1),
        owner_table,
        basis_up.astype(f32).reshape(-1),
        basis_down.astype(f32).reshape(-1),
        special_inverse,
        jnp.asarray(c1),
        jnp.asarray(np.ascontiguousarray(c1.T)),
        jnp.asarray(gram),
        root_keys.reshape((2, lm) + tile),
        switch_main,
        switch_special,
        jnp.asarray(table.astype(np.float32)),
        jnp.asarray((1.0 / table).astype(np.float32)),
    )
    return out.reshape((1, cap, 1, 2, lm) + tile)


def solution(mesh):
    sizes = [mesh.shape[axis] for axis in ("leaf", "limb", "coef")]
    return jax.shard_map(
        functools.partial(per_device, *sizes),
        mesh=mesh,
        in_specs=(
            P(("grp", "leaf"), None, None, "limb", "coef", None),
            P(("grp", "leaf"), None, None, None, "limb", "coef", None),
            P(("grp", "leaf"), None, None, None, "limb", "coef", None),
            P(),
            P("limb", None),
            P("limb"),
            P(None, "grp"),
            P("grp"),
        ),
        out_specs=P(("grp", "leaf"), None, None, None, "limb", "coef", None),
        check_vma=False,
    )
```

```python
import functools
import math

import jax
import jax.numpy as jnp
import ml_dtypes
import numpy as np
from jax import lax
from jax.experimental import pallas as pl
from jax.experimental.pallas import tpu as pltpu
from jax.sharding import PartitionSpec as P

MESH = pl.DeviceIdType.MESH
CHUNK = 3


def cosine_table(length):
    frequency = np.arange(length).astype(np.float32)[:, None]
    sample = np.arange(length).astype(np.float32)[None, :]
    weight = np.where(
        frequency == 0, np.sqrt(np.float32(1.0 / length)), np.sqrt(np.float32(2.0 / length))
    )
    angle = np.float32(math.pi) * (np.float32(2.0) * sample + np.float32(1.0)) * frequency
    angle = angle / np.float32(2.0 * length)
    return (weight * np.cos(angle)).astype(ml_dtypes.bfloat16)


def twist_table(limbs, n1, n2):
    product = (
        (2 * np.arange(limbs) + 1)[:, None, None]
        * np.arange(n2)[None, :, None]
        * np.arange(n1)[None, None, :]
        % n2
    )
    return 1.0 + 0.5 * np.cos(2.0 * math.pi * product / n2)


def dot(a, b):
    return jnp.dot(a, b, preferred_element_type=jnp.float32)


def pick(n, index, load):
    if n <= 8:
        value = load(0)
        for j in range(1, n):
            value = jnp.where(index == j, load(j), value)
        return value
    return lax.fori_loop(
        1, n, lambda j, value: jnp.where(index == j, load(j), value), load(0)
    )


def repeat(low, high, body):
    if high - low <= 8:
        for i in range(low, high):
            body(i)
    else:
        lax.fori_loop(low, high, lambda i, c: (body(i), c)[1], 0)


def kernel(
    cfg,
    parent_ref,
    owner_ref,
    up_ref,
    down_ref,
    inv_ref,
    c1_ref,
    c1t_ref,
    d_ref,
    root_ref,
    main_hbm,
    special_hbm,
    twist_hbm,
    recip_hbm,
    out_ref,
    main_key,
    special_key,
    twist,
    recip,
    z_buf,
    x_gather,
    b_gather,
    f_gather,
    x_buf,
    z2_buf,
    x2_buf,
    s_main,
    s_special,
    b_add,
    stage,
    up_f32,
    down_f32,
    up_smem,
    down_smem,
    load_sem,
    route_send,
    relay_send,
    route_recv,
    z_sem,
    x_send,
    x_recv,
    z2_sem,
    x2_send,
    x2_recv,
):
    n, nl, lm, ls, lq, lp, digits, levels, cap, half = cfg
    width = CHUNK
    chunks = lm // width
    me = lax.axis_index("leaf")
    limb = lax.axis_index("limb")
    coef = lax.axis_index("coef")
    other = 1 - coef

    loads = []
    for l in range(levels):
        loads.append(pltpu.make_async_copy(main_hbm.at[0, l], main_key.at[l], load_sem.at[l]))
        loads.append(
            pltpu.make_async_copy(special_hbm.at[0, l], special_key.at[l], load_sem.at[levels + l])
        )
    rows = pl.ds(pl.multiple_of(coef * half, half), half)
    tables = []
    for k, (src, dst) in enumerate(((recip_hbm, recip), (twist_hbm, twist))):
        tables.append(
            pltpu.make_async_copy(
                src.at[pl.ds(limb * lm, lm), rows], dst.at[pl.ds(0, lm)], load_sem.at[2 * levels + 2 * k]
            )
        )
        tables.append(
            pltpu.make_async_copy(
                src.at[pl.ds(lq + limb * ls, ls), rows],
                dst.at[pl.ds(lm, ls)],
                load_sem.at[2 * levels + 2 * k + 1],
            )
        )
    up_f32[...] = up_ref[...].astype(jnp.float32)
    down_f32[...] = down_ref[...].astype(jnp.float32)
    scalars = [
        pltpu.make_async_copy(up_f32, up_smem, load_sem.at[2 * levels + 4]),
        pltpu.make_async_copy(down_f32, down_smem, load_sem.at[2 * levels + 5]),
    ]
    for copy in tables + loads + scalars:
        copy.start()

    barrier = pltpu.get_barrier_semaphore()

    def greet(target):
        meets = (target > 0) & (target < n - 1) | (me > 0) & (me < n - 1)

        @pl.when((target != me) & meets)
        def _():
            pl.semaphore_signal(barrier, inc=1, device_id={"leaf": target}, device_id_type=MESH)

    repeat(0, n, greet)
    pl.semaphore_signal(barrier, inc=1, device_id={"coef": other}, device_id_type=MESH)
    for k in range(1, nl):
        pl.semaphore_signal(
            barrier, inc=1, device_id={"limb": lax.rem(limb + k, nl)}, device_id_type=MESH
        )
    at_end = (me == 0) | (me == n - 1)
    pl.semaphore_wait(barrier, nl + jnp.where(at_end, n - 2, n - 1))

    ends = ((n - 2, n - 1, 0), (1, 0, 1))
    inner = (me > 0) & (me < n - 1)

    class Route:
        def __init__(self, unit, buf, lead, width, whole):
            self.unit, self.buf, self.lead, self.width, self.whole = unit, buf, lead, width, whole
            self.chunks = lm // width

        def piece(self, slot, c):
            return self.buf.at[self.lead, slot, pl.ds(c * self.width, self.width)]

        def hop(self, slot, c, target):
            return pltpu.make_async_remote_copy(
                src_ref=self.piece(slot, c),
                dst_ref=self.piece(slot, c),
                send_sem=route_send.at[self.unit, target, c],
                recv_sem=route_recv.at[self.unit, slot, c],
                device_id={"leaf": target},
                device_id_type=MESH,
            )

        def relay(self, c, end, side, slot):
            if self.whole:
                source = self.piece(slot, c)
            else:
                source = stage.at[self.unit, side, pl.ds(c * self.width, self.width)]
            return pltpu.make_async_remote_copy(
                src_ref=source,
                dst_ref=self.piece(slot, c),
                send_sem=relay_send.at[self.unit, side, slot, c],
                recv_sem=route_recv.at[self.unit, slot, c],
                device_id={"leaf": end},
                device_id_type=MESH,
            )

        def start(self, c):
            def one(target):
                @pl.when(target != me)
                def _():
                    self.hop(me, c, target).start()

            if self.whole:
                for near, end, side in ends:

                    @pl.when(me == near)
                    def _():
                        self.relay(c, end, side, me).start()

            repeat(1, n - 1, one)

        def arrive(self, c, needed=None):
            @pl.when(inner)
            def _():
                def one(slot):
                    @pl.when(slot != me)
                    def _():
                        self.hop(slot, c, lax.rem(me + 1, n)).wait_recv()
                        if self.whole:
                            for near, end, side in ends:

                                @pl.when((me == near) & (slot != end))
                                def _():
                                    self.relay(c, end, side, slot).start()

                repeat(0, n, one)
                if not self.whole:
                    for near, end, side in ends:

                        @pl.when(me == near)
                        def _():
                            for t in range(c * self.width, (c + 1) * self.width):
                                stage[self.unit, side, t] = self.choose(needed[side], t)
                            self.relay(c, end, side, me).start()

        def settle(self, c):
            for near, end, side in ends:

                @pl.when(me == end)
                def _():
                    if self.whole:

                        def one(slot):
                            @pl.when(slot != end)
                            def _():
                                self.hop(slot, c, near).wait_recv()

                        repeat(0, n, one)
                    else:
                        self.hop(near, c, near).wait_recv()

        def choose(self, index, t):
            return pick(n, index, lambda j: self.buf[self.lead, j, t])

        def take(self, index, t, use):
            @pl.when(inner)
            def _():
                use(self.choose(index, t))

            for near, end, side in ends:

                @pl.when(me == end)
                def _():
                    own = self.buf[self.lead, end, t]
                    use(jnp.where(index == end, own, self.buf[self.lead, near, t]))

        def end(self):
            for c in range(self.chunks):

                def one(target):
                    @pl.when(target != me)
                    def _():
                        self.hop(me, c, target).wait_send()

                repeat(1, n - 1, one)
                for near, end, side in ends:

                    @pl.when(me == near)
                    def _():
                        if self.whole:

                            def other_slot(slot):
                                @pl.when(slot != end)
                                def _():
                                    self.relay(c, end, side, slot).wait_send()

                            repeat(0, n, other_slot)
                        else:
                            self.relay(c, end, side, me).wait_send()

    def part(c):
        return pl.ds(c * width, width)

    c1 = c1_ref[...]
    c1t = c1t_ref[...]
    d_own = d_ref[rows, :]

    def z_copy(buf, sem, l, c, where):
        return pltpu.make_async_remote_copy(
            src_ref=buf.at[l, coef, where],
            dst_ref=buf.at[l, coef, where],
            send_sem=sem.at[l, 0, c],
            recv_sem=sem.at[l, 1, c],
            device_id={"coef": other},
            device_id_type=MESH,
        )

    def mixed(buf, l, t):
        own = buf[l, coef, t].astype(jnp.float32)
        return own + dot(d_own[:, :half], buf[l, 0, t]) + dot(d_own[:, half:], buf[l, 1, t])

    def x_copy(l, c, k):
        return pltpu.make_async_remote_copy(
            src_ref=x_buf.at[l, limb, c],
            dst_ref=x_buf.at[l, limb, c],
            send_sem=x_send.at[l, c, k - 1],
            recv_sem=x_recv.at[l, c, k - 1],
            device_id={"limb": lax.rem(limb + k, nl)},
            device_id_type=MESH,
        )

    def x2_copy(l, k):
        return pltpu.make_async_remote_copy(
            src_ref=x2_buf.at[l, limb],
            dst_ref=x2_buf.at[l, limb],
            send_sem=x2_send.at[l, k - 1],
            recv_sem=x2_recv.at[l, k - 1],
            device_id={"limb": lax.rem(limb + k, nl)},
            device_id_type=MESH,
        )

    def switched(l, t_global, t_twist, key_of):
        sums = [None, None]
        w = twist[t_twist]
        for d in range(digits):
            total = None
            for s in range(CHUNK):
                at = d * CHUNK + s
                term = x_buf[l, at // lm, at % lm].astype(jnp.float32)
                term = term * up_smem[d, t_global, s]
                total = term if total is None else total + term
            hat = dot((total * w).astype(jnp.bfloat16), c1t)
            for i in range(2):
                add = hat * key_of(d, i).astype(jnp.float32)
                sums[i] = add if sums[i] is None else sums[i] + add
        return sums

    def corrected(l, i, q):
        total = None
        for p in range(lp):
            term = x2_buf[l, p // ls, i * ls + p % ls].astype(jnp.float32) * down_smem[q, p]
            total = term if total is None else total + term
        hat = dot((total * twist[q]).astype(jnp.bfloat16), c1t)
        return (s_main[i, q] - hat) * inv_ref[q]

    def put(buf, where, value):
        buf[where] = value

    def finish_b(l, use):
        way_b = ways[l][1]
        for c in range(chunks):
            way_b.settle(c)
            for t in range(c * width, (c + 1) * width):
                way_b.take(
                    parent_ref[l, me],
                    t,
                    lambda held: use(t, (held.astype(jnp.float32) + b_add[t]).astype(jnp.bfloat16)),
                )

    b_gather[0, me] = root_ref[0]
    tables[0].wait()
    tables[1].wait()

    def send_z(l, t, value):
        z_buf[l, coef, t] = (dot(value, c1) * recip[t]).astype(jnp.bfloat16)

    for c in range(chunks):
        for t in range(c * width, (c + 1) * width):
            send_z(0, t, root_ref[1, t])
        z_copy(z_buf, z_sem, 0, c, part(c)).start()
    tables[2].wait()
    tables[3].wait()

    ways = [
        (Route(2 * l, x_gather, l, 1, False), Route(2 * l + 1, b_gather, l, width, False))
        for l in range(levels)
    ]
    final = [Route(2 * levels + i, f_gather, i, width, True) for i in range(2)]

    for l in range(levels):
        parent = parent_ref[l, me]
        needed = (parent_ref[l, n - 1], parent_ref[l, 0])
        way_x, way_b = ways[l]
        for c in range(chunks):
            z_copy(z_buf, z_sem, l, c, part(c)).wait_recv()
            for t in range(c * width, (c + 1) * width):
                x_gather[l, me, t] = mixed(z_buf, l, t).astype(jnp.bfloat16)
                way_x.start(t)
        if l > 0:
            finish_b(l - 1, lambda t, value: put(b_gather, (l, me, t), value))
        for t in range(lm):
            way_x.arrive(t, needed)
            way_x.settle(t)
            way_x.take(parent, t, lambda value: put(x_buf, (l, limb, t), value))
            for k in range(1, nl):
                x_copy(l, t, k).start()
        for c in range(chunks):
            way_b.start(c)
        if l == 0:
            for copy in scalars:
                copy.wait()
        loads[2 * l].wait()
        loads[2 * l + 1].wait()
        for t in range(lm):
            for k in range(1, nl):
                x_copy(l, t, k).wait_recv()

        for p in range(ls):
            sums = switched(
                l, lq + limb * ls + p, lm + p, lambda d, i: special_key[l, d, i, p]
            )
            for i in range(2):
                z = dot(sums[i].astype(jnp.bfloat16), c1) * recip[lm + p]
                z2_buf[l, coef, i * ls + p] = z.astype(jnp.bfloat16)
        everything = pl.ds(0, 2 * ls)
        z_copy(z2_buf, z2_sem, l, 0, everything).start()
        z_copy(z2_buf, z2_sem, l, 0, everything).wait_recv()
        for e in range(2 * ls):
            x2_buf[l, limb, e] = mixed(z2_buf, l, e).astype(jnp.bfloat16)
        for k in range(1, nl):
            x2_copy(l, k).start()

        def main_target(t, carry):
            sums = switched(l, limb * lm + t, t, lambda d, i: main_key[l, d, i, t])
            s_main[0, t] = sums[0]
            s_main[1, t] = sums[1]
            return carry

        lax.fori_loop(0, lm, main_target, 0)
        for k in range(1, nl):
            x2_copy(l, k).wait_recv()

        last = l == levels - 1
        for c in range(chunks):
            for t in range(c * width, (c + 1) * width):
                value = corrected(l, 1, t).astype(jnp.bfloat16)
                if last:
                    f_gather[1, me, t] = value
                else:
                    send_z(l + 1, t, value)
            if last:
                final[1].start(c)
            else:
                z_copy(z_buf, z_sem, l + 1, c, part(c)).start()

        def b_part(t, carry):
            b_add[t] = corrected(l, 0, t)
            return carry

        lax.fori_loop(0, lm, b_part, 0)
        for c in range(chunks):
            way_b.arrive(c, needed)

    finish_b(levels - 1, lambda t, value: put(f_gather, (0, me, t), value))
    for c in range(chunks):
        final[0].start(c)
    for way in (final[1], final[0]):
        for c in range(chunks):
            way.arrive(c)
    for way in (final[1], final[0]):
        for c in range(chunks):
            way.settle(c)

    def seek(j, state):
        count, sources, found = state
        mine = (owner_ref[j] == me).astype(jnp.int32)
        hits = [mine * (count == s).astype(jnp.int32) for s in range(cap)]
        sources = tuple(src + hit * j for src, hit in zip(sources, hits))
        found = tuple(f + hit for f, hit in zip(found, hits))
        return count + mine, sources, found

    zero = jnp.int32(0)
    _, sources, found = lax.fori_loop(0, n, seek, (zero, (zero,) * cap, (zero,) * cap))
    for s in range(cap):
        for i in range(2):
            value = f_gather[i, sources[s]]
            out_ref[s, i] = jnp.where(found[s] > 0, value, jnp.zeros_like(value))

    for l in range(levels):
        for way in ways[l]:
            way.end()
        for c in range(chunks):
            z_copy(z_buf, z_sem, l, c, part(c)).wait_send()
        for t in range(lm):
            for k in range(1, nl):
                x_copy(l, t, k).wait_send()
        z_copy(z2_buf, z2_sem, l, 0, pl.ds(0, 2 * ls)).wait_send()
        for k in range(1, nl):
            x2_copy(l, k).wait_send()
    for way in final:
        way.end()


def per_device(
    n,
    nl,
    nc,
    root_keys,
    switch_main,
    switch_special,
    basis_up,
    basis_down,
    special_inverse,
    parent_table,
    owner_table,
):
    cap = 3
    _, levels, digits, _, lm, half, n1 = switch_main.shape
    ls = switch_special.shape[4]
    lq, lp = lm * nl, ls * nl
    n2 = half * nc
    chunks = lm // CHUNK
    c1 = cosine_table(n1)
    c2 = cosine_table(n2).astype(np.float64)
    gram = (c2 @ c2.T - np.eye(n2)).astype(np.float32).astype(ml_dtypes.bfloat16)
    table = twist_table(lq + lp, n1, n2)
    cfg = (n, nl, lm, ls, lq, lp, digits, levels, cap, half)
    bf16, f32 = jnp.bfloat16, jnp.float32
    tile = (half, n1)
    smem = pl.BlockSpec(memory_space=pltpu.SMEM)
    vmem = pl.BlockSpec(memory_space=pltpu.VMEM)
    hbm = pl.BlockSpec(memory_space=pl.ANY)
    dma = pltpu.SemaphoreType.DMA
    units = 2 * levels + 2
    out = pl.pallas_call(
        functools.partial(kernel, cfg),
        out_shape=jax.ShapeDtypeStruct((cap, 2, lm) + tile, bf16),
        in_specs=[smem] * 2 + [vmem] * 2 + [smem] + [vmem] * 4 + [hbm] * 4,
        out_specs=vmem,
        scratch_shapes=[
            pltpu.VMEM((levels, digits, 2, lm) + tile, bf16),
            pltpu.VMEM((levels, digits, 2, ls) + tile, bf16),
            pltpu.VMEM((lm + ls,) + tile, f32),
            pltpu.VMEM((lm + ls,) + tile, f32),
            pltpu.VMEM((levels, 2, lm) + tile, bf16),
            pltpu.VMEM((levels, n, lm) + tile, bf16),
            pltpu.VMEM((levels, n, lm) + tile, bf16),
            pltpu.VMEM((2, n, lm) + tile, bf16),
            pltpu.VMEM((levels, nl, lm) + tile, bf16),
            pltpu.VMEM((levels, 2, 2 * ls) + tile, bf16),
            pltpu.VMEM((levels, nl, 2 * ls) + tile, bf16),
            pltpu.VMEM((2, lm) + tile, f32),
            pltpu.VMEM((2, ls) + tile, f32),
            pltpu.VMEM((lm,) + tile, f32),
            pltpu.VMEM((2 * levels, 2, lm) + tile, bf16),
            pltpu.VMEM(basis_up.shape, f32),
            pltpu.VMEM(basis_down.shape, f32),
            pltpu.SMEM(basis_up.shape, f32),
            pltpu.SMEM(basis_down.shape, f32),
            dma((2 * levels + 6,)),
            dma((units, n, lm)),
            dma((units, 2, n, lm)),
            dma((units, n, lm)),
            dma((levels, 2, chunks)),
            dma((levels, lm, nl - 1)),
            dma((levels, lm, nl - 1)),
            dma((levels, 2, 1)),
            dma((levels, nl - 1)),
            dma((levels, nl - 1)),
        ],
        compiler_params=pltpu.CompilerParams(
            collective_id=0, has_side_effects=True, vmem_limit_bytes=56 * 1024 * 1024
        ),
        name="derive_and_deliver",
    )(
        parent_table,
        owner_table,
        basis_up,
        basis_down,
        special_inverse,
        jnp.asarray(c1),
        jnp.asarray(np.ascontiguousarray(c1.T)),
        jnp.asarray(gram),
        root_keys.reshape((2, lm) + tile),
        switch_main,
        switch_special,
        jnp.asarray(table.astype(np.float32)),
        jnp.asarray((1.0 / table).astype(np.float32)),
    )
    return out.reshape((1, cap, 1, 2, lm) + tile)


def solution(mesh):
    sizes = [mesh.shape[axis] for axis in ("leaf", "limb", "coef")]
    return jax.shard_map(
        functools.partial(per_device, *sizes),
        mesh=mesh,
        in_specs=(
            P(("grp", "leaf"), None, None, "limb", "coef", None),
            P(("grp", "leaf"), None, None, None, "limb", "coef", None),
            P(("grp", "leaf"), None, None, None, "limb", "coef", None),
            P(),
            P("limb", None),
            P("limb"),
            P(None, "grp"),
            P("grp"),
        ),
        out_specs=P(("grp", "leaf"), None, None, None, "limb", "coef", None),
        check_vma=False,
    )
```

```python
import functools
import math

import jax
import jax.numpy as jnp
import ml_dtypes
import numpy as np
from jax import lax
from jax.experimental import pallas as pl
from jax.experimental.pallas import tpu as pltpu
from jax.sharding import PartitionSpec as P

MESH = pl.DeviceIdType.MESH
CHUNK = 3


def cosine_table(length):
    frequency = np.arange(length).astype(np.float32)[:, None]
    sample = np.arange(length).astype(np.float32)[None, :]
    weight = np.where(
        frequency == 0, np.sqrt(np.float32(1.0 / length)), np.sqrt(np.float32(2.0 / length))
    )
    angle = np.float32(math.pi) * (np.float32(2.0) * sample + np.float32(1.0)) * frequency
    angle = angle / np.float32(2.0 * length)
    return (weight * np.cos(angle)).astype(ml_dtypes.bfloat16)


def twist_table(limbs, n1, n2):
    product = (
        (2 * np.arange(limbs) + 1)[:, None, None]
        * np.arange(n2)[None, :, None]
        * np.arange(n1)[None, None, :]
        % n2
    )
    return 1.0 + 0.5 * np.cos(2.0 * math.pi * product / n2)


def dot(a, b):
    return jnp.dot(a, b, preferred_element_type=jnp.float32)


def pick(n, index, load):
    if n <= 8:
        value = load(0)
        for j in range(1, n):
            value = jnp.where(index == j, load(j), value)
        return value
    return lax.fori_loop(
        1, n, lambda j, value: jnp.where(index == j, load(j), value), load(0)
    )


def repeat(low, high, body):
    if high - low <= 8:
        for i in range(low, high):
            body(i)
    else:
        lax.fori_loop(low, high, lambda i, c: (body(i), c)[1], 0)


def kernel(
    cfg,
    parent_ref,
    up_ref,
    down_ref,
    inv_ref,
    c1_ref,
    c1t_ref,
    d_ref,
    root_ref,
    main_hbm,
    special_hbm,
    twist_hbm,
    recip_hbm,
    out_ref,
    main_key,
    special_key,
    twist,
    recip,
    z_buf,
    x_gather,
    b_gather,
    f_gather,
    x_buf,
    z2_buf,
    x2_buf,
    s_main,
    s_special,
    b_add,
    stage,
    up_f32,
    down_f32,
    up_smem,
    down_smem,
    load_sem,
    store_sem,
    route_send,
    relay_send,
    route_recv,
    z_sem,
    x_send,
    x_recv,
    z2_sem,
    x2_send,
    x2_recv,
):
    n, nl, lm, ls, lq, lp, digits, levels, cap, half = cfg
    width = CHUNK
    chunks = lm // width
    me = lax.axis_index("leaf")
    limb = lax.axis_index("limb")
    coef = lax.axis_index("coef")
    other = 1 - coef

    loads = []
    for l in range(levels):
        loads.append(pltpu.make_async_copy(main_hbm.at[0, l], main_key.at[l], load_sem.at[l]))
        loads.append(
            pltpu.make_async_copy(special_hbm.at[0, l], special_key.at[l], load_sem.at[levels + l])
        )
    rows = pl.ds(pl.multiple_of(coef * half, half), half)
    tables = []
    for k, (src, dst) in enumerate(((recip_hbm, recip), (twist_hbm, twist))):
        tables.append(
            pltpu.make_async_copy(
                src.at[pl.ds(limb * lm, lm), rows], dst.at[pl.ds(0, lm)], load_sem.at[2 * levels + 2 * k]
            )
        )
        tables.append(
            pltpu.make_async_copy(
                src.at[pl.ds(lq + limb * ls, ls), rows],
                dst.at[pl.ds(lm, ls)],
                load_sem.at[2 * levels + 2 * k + 1],
            )
        )
    up_f32[...] = up_ref[...].astype(jnp.float32)
    down_f32[...] = down_ref[...].astype(jnp.float32)
    scalars = [
        pltpu.make_async_copy(up_f32, up_smem, load_sem.at[2 * levels + 4]),
        pltpu.make_async_copy(down_f32, down_smem, load_sem.at[2 * levels + 5]),
    ]
    for copy in tables + loads + scalars:
        copy.start()

    barrier = pltpu.get_barrier_semaphore()

    def greet(target):
        meets = (target > 0) & (target < n - 1) | (me > 0) & (me < n - 1)

        @pl.when((target != me) & meets)
        def _():
            pl.semaphore_signal(barrier, inc=1, device_id={"leaf": target}, device_id_type=MESH)

    repeat(0, n, greet)
    pl.semaphore_signal(barrier, inc=1, device_id={"coef": other}, device_id_type=MESH)
    for k in range(1, nl):
        pl.semaphore_signal(
            barrier, inc=1, device_id={"limb": lax.rem(limb + k, nl)}, device_id_type=MESH
        )
    at_end = (me == 0) | (me == n - 1)
    pl.semaphore_wait(barrier, nl + jnp.where(at_end, n - 2, n - 1))

    ends = ((n - 2, n - 1, 0), (1, 0, 1))
    inner = (me > 0) & (me < n - 1)

    class Route:
        def __init__(self, unit, buf, lead, width, whole):
            self.unit, self.buf, self.lead, self.width, self.whole = unit, buf, lead, width, whole
            self.chunks = lm // width

        def piece(self, slot, c):
            return self.buf.at[self.lead, slot, pl.ds(c * self.width, self.width)]

        def hop(self, slot, c, target):
            return pltpu.make_async_remote_copy(
                src_ref=self.piece(slot, c),
                dst_ref=self.piece(slot, c),
                send_sem=route_send.at[self.unit, target, c],
                recv_sem=route_recv.at[self.unit, slot, c],
                device_id={"leaf": target},
                device_id_type=MESH,
            )

        def relay(self, c, end, side, slot):
            if self.whole:
                source = self.piece(slot, c)
            else:
                source = stage.at[self.unit, side, pl.ds(c * self.width, self.width)]
            return pltpu.make_async_remote_copy(
                src_ref=source,
                dst_ref=self.piece(slot, c),
                send_sem=relay_send.at[self.unit, side, slot, c],
                recv_sem=route_recv.at[self.unit, slot, c],
                device_id={"leaf": end},
                device_id_type=MESH,
            )

        def start(self, c):
            def one(target):
                @pl.when(target != me)
                def _():
                    self.hop(me, c, target).start()

            if self.whole:
                for near, end, side in ends:

                    @pl.when(me == near)
                    def _():
                        self.relay(c, end, side, me).start()

            repeat(1, n - 1, one)

        def arrive(self, c, needed=None):
            @pl.when(inner)
            def _():
                def one(slot):
                    @pl.when(slot != me)
                    def _():
                        self.hop(slot, c, lax.rem(me + 1, n)).wait_recv()
                        if self.whole:
                            for near, end, side in ends:

                                @pl.when((me == near) & (slot != end))
                                def _():
                                    self.relay(c, end, side, slot).start()

                repeat(0, n, one)
                if not self.whole:
                    for near, end, side in ends:

                        @pl.when(me == near)
                        def _():
                            for t in range(c * self.width, (c + 1) * self.width):
                                stage[self.unit, side, t] = self.choose(needed[side], t)
                            self.relay(c, end, side, me).start()

        def settle(self, c):
            for near, end, side in ends:

                @pl.when(me == end)
                def _():
                    if self.whole:

                        def one(slot):
                            @pl.when(slot != end)
                            def _():
                                self.hop(slot, c, near).wait_recv()

                        repeat(0, n, one)
                    else:
                        self.hop(near, c, near).wait_recv()

        def choose(self, index, t):
            return pick(n, index, lambda j: self.buf[self.lead, j, t])

        def take(self, index, t, use):
            @pl.when(inner)
            def _():
                use(self.choose(index, t))

            for near, end, side in ends:

                @pl.when(me == end)
                def _():
                    own = self.buf[self.lead, end, t]
                    use(jnp.where(index == end, own, self.buf[self.lead, near, t]))

        def end(self):
            for c in range(self.chunks):

                def one(target):
                    @pl.when(target != me)
                    def _():
                        self.hop(me, c, target).wait_send()

                repeat(1, n - 1, one)
                for near, end, side in ends:

                    @pl.when(me == near)
                    def _():
                        if self.whole:

                            def other_slot(slot):
                                @pl.when(slot != end)
                                def _():
                                    self.relay(c, end, side, slot).wait_send()

                            repeat(0, n, other_slot)
                        else:
                            self.relay(c, end, side, me).wait_send()

    def part(c):
        return pl.ds(c * width, width)

    c1 = c1_ref[...]
    c1t = c1t_ref[...]
    d_own = d_ref[rows, :]

    def z_copy(buf, sem, l, c, where):
        return pltpu.make_async_remote_copy(
            src_ref=buf.at[l, coef, where],
            dst_ref=buf.at[l, coef, where],
            send_sem=sem.at[l, 0, c],
            recv_sem=sem.at[l, 1, c],
            device_id={"coef": other},
            device_id_type=MESH,
        )

    def mixed(buf, l, t):
        own = buf[l, coef, t].astype(jnp.float32)
        return own + dot(d_own[:, :half], buf[l, 0, t]) + dot(d_own[:, half:], buf[l, 1, t])

    def x_copy(l, c, k):
        return pltpu.make_async_remote_copy(
            src_ref=x_buf.at[l, limb, c],
            dst_ref=x_buf.at[l, limb, c],
            send_sem=x_send.at[l, c, k - 1],
            recv_sem=x_recv.at[l, c, k - 1],
            device_id={"limb": lax.rem(limb + k, nl)},
            device_id_type=MESH,
        )

    def x2_copy(l, k):
        return pltpu.make_async_remote_copy(
            src_ref=x2_buf.at[l, limb],
            dst_ref=x2_buf.at[l, limb],
            send_sem=x2_send.at[l, k - 1],
            recv_sem=x2_recv.at[l, k - 1],
            device_id={"limb": lax.rem(limb + k, nl)},
            device_id_type=MESH,
        )

    def switched(l, t_global, t_twist, key_of):
        w = twist[t_twist]
        turned = []
        for d in range(digits):
            total = None
            for s in range(CHUNK):
                at = d * CHUNK + s
                term = x_buf[l, at // lm, at % lm].astype(jnp.float32)
                term = term * up_smem[s, d, t_global]
                total = term if total is None else total + term
            turned.append((total * w).astype(jnp.bfloat16))
        hats = dot(jnp.concatenate(turned, axis=0), c1t)
        sums = [None, None]
        for d in range(digits):
            hat = hats[d * half : (d + 1) * half]
            for i in range(2):
                add = hat * key_of(d, i).astype(jnp.float32)
                sums[i] = add if sums[i] is None else sums[i] + add
        return sums

    def corrected(l, i, q):
        total = None
        for p in range(lp):
            term = x2_buf[l, p // ls, i * ls + p % ls].astype(jnp.float32) * down_smem[p, q]
            total = term if total is None else total + term
        hat = dot((total * twist[q]).astype(jnp.bfloat16), c1t)
        return (s_main[i, q] - hat) * inv_ref[q]

    def put(buf, where, value):
        buf[where] = value

    def finish_b(l, use):
        way_b = ways[l][1]

        def b_part(c, carry):
            for t in range(width):
                b_add[c * width + t] = corrected(l, 0, c * width + t)
            return carry

        lax.fori_loop(0, chunks, b_part, 0)
        for c in range(chunks):
            way_b.arrive(c, (parent_ref[l, n - 1], parent_ref[l, 0]))
            way_b.settle(c)
            for t in range(c * width, (c + 1) * width):
                way_b.take(
                    parent_ref[l, me],
                    t,
                    lambda held: use(t, (held.astype(jnp.float32) + b_add[t]).astype(jnp.bfloat16)),
                )

    b_gather[0, me] = root_ref[0]
    tables[0].wait()
    tables[1].wait()

    def send_z(l, t, value):
        z_buf[l, coef, t] = (dot(value, c1) * recip[t]).astype(jnp.bfloat16)

    for c in range(chunks):
        for t in range(c * width, (c + 1) * width):
            send_z(0, t, root_ref[1, t])
        z_copy(z_buf, z_sem, 0, c, part(c)).start()
    tables[2].wait()
    tables[3].wait()

    ways = [
        (Route(2 * l, x_gather, l, 1, False), Route(2 * l + 1, b_gather, l, width, False))
        for l in range(levels)
    ]
    final = [Route(2 * levels + i, f_gather, i, width, True) for i in range(2)]

    for l in range(levels):
        parent = parent_ref[l, me]
        needed = (parent_ref[l, n - 1], parent_ref[l, 0])
        way_x, way_b = ways[l]
        for c in range(chunks):
            z_copy(z_buf, z_sem, l, c, part(c)).wait_recv()
            for t in range(c * width, (c + 1) * width):
                x_gather[l, me, t] = mixed(z_buf, l, t).astype(jnp.bfloat16)
                way_x.start(t)
        if l > 0:
            finish_b(l - 1, lambda t, value: put(b_gather, (l, me, t), value))
        for t in range(lm):
            way_x.arrive(t, needed)
            way_x.settle(t)
            way_x.take(parent, t, lambda value: put(x_buf, (l, limb, t), value))
            for k in range(1, nl):
                x_copy(l, t, k).start()
        for c in range(chunks):
            way_b.start(c)
        if l == 0:
            for copy in scalars:
                copy.wait()
        loads[2 * l].wait()
        loads[2 * l + 1].wait()
        for t in range(lm):
            for k in range(1, nl):
                x_copy(l, t, k).wait_recv()

        for p in range(ls):
            sums = switched(
                l, lq + limb * ls + p, lm + p, lambda d, i: special_key[l, d, i, p]
            )
            for i in range(2):
                z = dot(sums[i].astype(jnp.bfloat16), c1) * recip[lm + p]
                z2_buf[l, coef, i * ls + p] = z.astype(jnp.bfloat16)
        everything = pl.ds(0, 2 * ls)
        z_copy(z2_buf, z2_sem, l, 0, everything).start()
        z_copy(z2_buf, z2_sem, l, 0, everything).wait_recv()
        for e in range(2 * ls):
            x2_buf[l, limb, e] = mixed(z2_buf, l, e).astype(jnp.bfloat16)
        for k in range(1, nl):
            x2_copy(l, k).start()

        def main_targets(c, carry):
            for t in range(width):
                at = c * width + t
                sums = switched(l, limb * lm + at, at, lambda d, i: main_key[l, d, i, at])
                s_main[0, at] = sums[0]
                s_main[1, at] = sums[1]
            return carry

        lax.fori_loop(0, chunks, main_targets, 0)
        for k in range(1, nl):
            x2_copy(l, k).wait_recv()

        last = l == levels - 1
        for c in range(chunks):
            for t in range(c * width, (c + 1) * width):
                value = corrected(l, 1, t).astype(jnp.bfloat16)
                if last:
                    f_gather[1, me, t] = value
                else:
                    send_z(l + 1, t, value)
            if last:
                final[1].start(c)
            else:
                z_copy(z_buf, z_sem, l + 1, c, part(c)).start()

    finish_b(levels - 1, lambda t, value: put(f_gather, (0, me, t), value))
    for c in range(chunks):
        final[0].start(c)
    def store(i, c):
        def one(slot):
            pltpu.make_async_copy(
                final[i].piece(slot, c),
                out_ref.at[i, slot, part(c)],
                store_sem.at[i, slot, c],
            ).start()

        repeat(0, n, one)

    for i in (1, 0):
        for c in range(chunks):
            final[i].arrive(c)
    for i in (1, 0):
        for c in range(chunks):
            final[i].settle(c)
            store(i, c)
    for i in (1, 0):
        for c in range(chunks):

            def stored(slot):
                pltpu.make_async_copy(
                    final[i].piece(slot, c),
                    out_ref.at[i, slot, part(c)],
                    store_sem.at[i, slot, c],
                ).wait()

            repeat(0, n, stored)

    for l in range(levels):
        for way in ways[l]:
            way.end()
        for c in range(chunks):
            z_copy(z_buf, z_sem, l, c, part(c)).wait_send()
        for t in range(lm):
            for k in range(1, nl):
                x_copy(l, t, k).wait_send()
        z_copy(z2_buf, z2_sem, l, 0, pl.ds(0, 2 * ls)).wait_send()
        for k in range(1, nl):
            x2_copy(l, k).wait_send()
    for way in final:
        way.end()


def deliver(n, cap, owner_ref, keys_ref, out_ref, zeros, sem):
    me = lax.axis_index("leaf")
    zeros[...] = jnp.zeros_like(zeros)

    def seek(j, state):
        count, sources, found = state
        mine = (owner_ref[j] == me).astype(jnp.int32)
        hits = [mine * (count == s).astype(jnp.int32) for s in range(cap)]
        sources = tuple(src + hit * j for src, hit in zip(sources, hits))
        found = tuple(f + hit for f, hit in zip(found, hits))
        return count + mine, sources, found

    zero = jnp.int32(0)
    _, sources, found = lax.fori_loop(0, n, seek, (zero, (zero,) * cap, (zero,) * cap))
    for s in range(cap):
        for i in range(2):

            @pl.when(found[s] > 0)
            def _():
                pltpu.make_async_copy(
                    keys_ref.at[i, sources[s]], out_ref.at[s, i], sem.at[s, i]
                ).start()

            @pl.when(found[s] == 0)
            def _():
                pltpu.make_async_copy(zeros, out_ref.at[s, i], sem.at[s, i]).start()

    for s in range(cap):
        for i in range(2):
            pltpu.make_async_copy(zeros, out_ref.at[s, i], sem.at[s, i]).wait()


def per_device(
    n,
    nl,
    nc,
    root_keys,
    switch_main,
    switch_special,
    basis_up,
    basis_down,
    special_inverse,
    parent_table,
    owner_table,
):
    cap = 3
    _, levels, digits, _, lm, half, n1 = switch_main.shape
    ls = switch_special.shape[4]
    lq, lp = lm * nl, ls * nl
    n2 = half * nc
    chunks = lm // CHUNK
    c1 = cosine_table(n1)
    c2 = cosine_table(n2).astype(np.float64)
    gram = (c2 @ c2.T - np.eye(n2)).astype(np.float32).astype(ml_dtypes.bfloat16)
    table = twist_table(lq + lp, n1, n2)
    basis_up = basis_up.transpose(2, 0, 1)
    basis_down = basis_down.T
    cfg = (n, nl, lm, ls, lq, lp, digits, levels, cap, half)
    bf16, f32 = jnp.bfloat16, jnp.float32
    tile = (half, n1)
    smem = pl.BlockSpec(memory_space=pltpu.SMEM)
    vmem = pl.BlockSpec(memory_space=pltpu.VMEM)
    hbm = pl.BlockSpec(memory_space=pl.ANY)
    dma = pltpu.SemaphoreType.DMA
    units = 2 * levels + 2
    keys = pl.pallas_call(
        functools.partial(kernel, cfg),
        out_shape=jax.ShapeDtypeStruct((2, n, lm) + tile, bf16),
        in_specs=[smem, vmem, vmem, smem] + [vmem] * 4 + [hbm] * 4,
        out_specs=hbm,
        scratch_shapes=[
            pltpu.VMEM((levels, digits, 2, lm) + tile, bf16),
            pltpu.VMEM((levels, digits, 2, ls) + tile, bf16),
            pltpu.VMEM((lm + ls,) + tile, f32),
            pltpu.VMEM((lm + ls,) + tile, f32),
            pltpu.VMEM((levels, 2, lm) + tile, bf16),
            pltpu.VMEM((levels, n, lm) + tile, bf16),
            pltpu.VMEM((levels, n, lm) + tile, bf16),
            pltpu.VMEM((2, n, lm) + tile, bf16),
            pltpu.VMEM((levels, nl, lm) + tile, bf16),
            pltpu.VMEM((levels, 2, 2 * ls) + tile, bf16),
            pltpu.VMEM((levels, nl, 2 * ls) + tile, bf16),
            pltpu.VMEM((2, lm) + tile, f32),
            pltpu.VMEM((2, ls) + tile, f32),
            pltpu.VMEM((lm,) + tile, f32),
            pltpu.VMEM((2 * levels, 2, lm) + tile, bf16),
            pltpu.VMEM(basis_up.shape, f32),
            pltpu.VMEM(basis_down.shape, f32),
            pltpu.SMEM(basis_up.shape, f32),
            pltpu.SMEM(basis_down.shape, f32),
            dma((2 * levels + 6,)),
            dma((2, n, chunks)),
            dma((units, n, lm)),
            dma((units, 2, n, lm)),
            dma((units, n, lm)),
            dma((levels, 2, chunks)),
            dma((levels, lm, nl - 1)),
            dma((levels, lm, nl - 1)),
            dma((levels, 2, 1)),
            dma((levels, nl - 1)),
            dma((levels, nl - 1)),
        ],
        compiler_params=pltpu.CompilerParams(
            collective_id=0, has_side_effects=True, vmem_limit_bytes=56 * 1024 * 1024
        ),
        name="derive_and_deliver",
    )(
        parent_table,
        basis_up,
        basis_down,
        special_inverse,
        jnp.asarray(c1),
        jnp.asarray(np.ascontiguousarray(c1.T)),
        jnp.asarray(gram),
        root_keys.reshape((2, lm) + tile),
        switch_main,
        switch_special,
        jnp.asarray(table.astype(np.float32)),
        jnp.asarray((1.0 / table).astype(np.float32)),
    )
    out = pl.pallas_call(
        functools.partial(deliver, n, cap),
        out_shape=jax.ShapeDtypeStruct((cap, 2, lm) + tile, bf16),
        in_specs=[smem, hbm],
        out_specs=hbm,
        scratch_shapes=[pltpu.VMEM((lm,) + tile, bf16), dma((cap, 2))],
        compiler_params=pltpu.CompilerParams(vmem_limit_bytes=56 * 1024 * 1024),
        name="deliver",
    )(owner_table, keys)
    return out.reshape((1, cap, 1, 2, lm) + tile)


def solution(mesh):
    sizes = [mesh.shape[axis] for axis in ("leaf", "limb", "coef")]
    return jax.shard_map(
        functools.partial(per_device, *sizes),
        mesh=mesh,
        in_specs=(
            P(("grp", "leaf"), None, None, "limb", "coef", None),
            P(("grp", "leaf"), None, None, None, "limb", "coef", None),
            P(("grp", "leaf"), None, None, None, "limb", "coef", None),
            P(),
            P("limb", None),
            P("limb"),
            P(None, "grp"),
            P("grp"),
        ),
        out_specs=P(("grp", "leaf"), None, None, None, "limb", "coef", None),
        check_vma=False,
    )
```

```python
import functools
import math

import jax
import jax.numpy as jnp
import ml_dtypes
import numpy as np
from jax import lax
from jax.experimental import pallas as pl
from jax.experimental.pallas import tpu as pltpu
from jax.sharding import PartitionSpec as P

MESH = pl.DeviceIdType.MESH
CHUNK = 3


def cosine_table(length):
    frequency = np.arange(length).astype(np.float32)[:, None]
    sample = np.arange(length).astype(np.float32)[None, :]
    weight = np.where(
        frequency == 0, np.sqrt(np.float32(1.0 / length)), np.sqrt(np.float32(2.0 / length))
    )
    angle = np.float32(math.pi) * (np.float32(2.0) * sample + np.float32(1.0)) * frequency
    angle = angle / np.float32(2.0 * length)
    return (weight * np.cos(angle)).astype(ml_dtypes.bfloat16)


def twist_table(limbs, n1, n2):
    product = (
        (2 * np.arange(limbs) + 1)[:, None, None]
        * np.arange(n2)[None, :, None]
        * np.arange(n1)[None, None, :]
        % n2
    )
    return 1.0 + 0.5 * np.cos(2.0 * math.pi * product / n2)


def dot(a, b):
    return jnp.dot(a, b, preferred_element_type=jnp.float32)


def pick(n, index, load):
    if n <= 8:
        value = load(0)
        for j in range(1, n):
            value = jnp.where(index == j, load(j), value)
        return value
    return lax.fori_loop(
        1, n, lambda j, value: jnp.where(index == j, load(j), value), load(0)
    )


def repeat(low, high, body):
    if high - low <= 8:
        for i in range(low, high):
            body(i)
    else:
        lax.fori_loop(low, high, lambda i, c: (body(i), c)[1], 0)


def kernel(
    cfg,
    parent_ref,
    up_ref,
    down_ref,
    inv_ref,
    c1_ref,
    c1t_ref,
    d_ref,
    root_ref,
    main_hbm,
    special_hbm,
    twist_hbm,
    recip_hbm,
    out_ref,
    main_key,
    special_key,
    twist,
    recip,
    z_buf,
    x_gather,
    b_gather,
    f_gather,
    x_buf,
    z2_buf,
    x2_buf,
    s_main,
    s_special,
    b_add,
    stage,
    up_f32,
    down_f32,
    up_smem,
    down_smem,
    load_sem,
    store_sem,
    route_send,
    relay_send,
    route_recv,
    z_sem,
    x_send,
    x_recv,
    z2_sem,
    x2_send,
    x2_recv,
):
    n, nl, lm, ls, lq, lp, digits, levels, cap, half = cfg
    width = CHUNK
    chunks = lm // width
    me = lax.axis_index("leaf")
    limb = lax.axis_index("limb")
    coef = lax.axis_index("coef")
    other = 1 - coef

    loads = []
    for l in range(levels):
        loads.append(pltpu.make_async_copy(main_hbm.at[0, l], main_key.at[l], load_sem.at[l]))
        loads.append(
            pltpu.make_async_copy(special_hbm.at[0, l], special_key.at[l], load_sem.at[levels + l])
        )
    rows = pl.ds(pl.multiple_of(coef * half, half), half)
    tables = []
    for k, (src, dst) in enumerate(((recip_hbm, recip), (twist_hbm, twist))):
        tables.append(
            pltpu.make_async_copy(
                src.at[pl.ds(limb * lm, lm), rows], dst.at[pl.ds(0, lm)], load_sem.at[2 * levels + 2 * k]
            )
        )
        tables.append(
            pltpu.make_async_copy(
                src.at[pl.ds(lq + limb * ls, ls), rows],
                dst.at[pl.ds(lm, ls)],
                load_sem.at[2 * levels + 2 * k + 1],
            )
        )
    up_f32[...] = up_ref[...].astype(jnp.float32)
    down_f32[...] = down_ref[...].astype(jnp.float32)
    scalars = [
        pltpu.make_async_copy(up_f32, up_smem, load_sem.at[2 * levels + 4]),
        pltpu.make_async_copy(down_f32, down_smem, load_sem.at[2 * levels + 5]),
    ]
    for copy in tables + loads + scalars:
        copy.start()

    barrier = pltpu.get_barrier_semaphore()

    def greet(target):
        meets = (target > 0) & (target < n - 1) | (me > 0) & (me < n - 1)

        @pl.when((target != me) & meets)
        def _():
            pl.semaphore_signal(barrier, inc=1, device_id={"leaf": target}, device_id_type=MESH)

    repeat(0, n, greet)
    pl.semaphore_signal(barrier, inc=1, device_id={"coef": other}, device_id_type=MESH)
    for k in range(1, nl):
        pl.semaphore_signal(
            barrier, inc=1, device_id={"limb": lax.rem(limb + k, nl)}, device_id_type=MESH
        )
    at_end = (me == 0) | (me == n - 1)
    pl.semaphore_wait(barrier, nl + jnp.where(at_end, n - 2, n - 1))

    ends = ((n - 2, n - 1, 0), (1, 0, 1))
    inner = (me > 0) & (me < n - 1)

    class Route:
        def __init__(self, unit, buf, lead, width, whole):
            self.unit, self.buf, self.lead, self.width, self.whole = unit, buf, lead, width, whole
            self.chunks = lm // width

        def piece(self, slot, c):
            return self.buf.at[self.lead, slot, pl.ds(c * self.width, self.width)]

        def hop(self, slot, c, target):
            return pltpu.make_async_remote_copy(
                src_ref=self.piece(slot, c),
                dst_ref=self.piece(slot, c),
                send_sem=route_send.at[self.unit, target, c],
                recv_sem=route_recv.at[self.unit, slot, c],
                device_id={"leaf": target},
                device_id_type=MESH,
            )

        def relay(self, c, end, side, slot):
            if self.whole:
                source = self.piece(slot, c)
            else:
                source = stage.at[self.unit, side, pl.ds(c * self.width, self.width)]
            return pltpu.make_async_remote_copy(
                src_ref=source,
                dst_ref=self.piece(slot, c),
                send_sem=relay_send.at[self.unit, side, slot, c],
                recv_sem=route_recv.at[self.unit, slot, c],
                device_id={"leaf": end},
                device_id_type=MESH,
            )

        def start(self, c):
            def one(target):
                @pl.when(target != me)
                def _():
                    self.hop(me, c, target).start()

            if self.whole:
                for near, end, side in ends:

                    @pl.when(me == near)
                    def _():
                        self.relay(c, end, side, me).start()

            repeat(1, n - 1, one)

        def arrive(self, c, needed=None):
            @pl.when(inner)
            def _():
                def one(slot):
                    @pl.when(slot != me)
                    def _():
                        self.hop(slot, c, lax.rem(me + 1, n)).wait_recv()
                        if self.whole:
                            for near, end, side in ends:

                                @pl.when((me == near) & (slot != end))
                                def _():
                                    self.relay(c, end, side, slot).start()

                repeat(0, n, one)
                if not self.whole:
                    for near, end, side in ends:

                        @pl.when(me == near)
                        def _():
                            for t in range(c * self.width, (c + 1) * self.width):
                                stage[self.unit, side, t] = self.choose(needed[side], t)
                            self.relay(c, end, side, me).start()

        def settle(self, c):
            for near, end, side in ends:

                @pl.when(me == end)
                def _():
                    if self.whole:

                        def one(slot):
                            @pl.when(slot != end)
                            def _():
                                self.hop(slot, c, near).wait_recv()

                        repeat(0, n, one)
                    else:
                        self.hop(near, c, near).wait_recv()

        def choose(self, index, t):
            return pick(n, index, lambda j: self.buf[self.lead, j, t])

        def take(self, index, t, use):
            @pl.when(inner)
            def _():
                use(self.choose(index, t))

            for near, end, side in ends:

                @pl.when(me == end)
                def _():
                    own = self.buf[self.lead, end, t]
                    use(jnp.where(index == end, own, self.buf[self.lead, near, t]))

        def end(self):
            for c in range(self.chunks):

                def one(target):
                    @pl.when(target != me)
                    def _():
                        self.hop(me, c, target).wait_send()

                repeat(1, n - 1, one)
                for near, end, side in ends:

                    @pl.when(me == near)
                    def _():
                        if self.whole:

                            def other_slot(slot):
                                @pl.when(slot != end)
                                def _():
                                    self.relay(c, end, side, slot).wait_send()

                            repeat(0, n, other_slot)
                        else:
                            self.relay(c, end, side, me).wait_send()

    def part(c):
        return pl.ds(c * width, width)

    c1 = c1_ref[...]
    c1t = c1t_ref[...]
    d_own = d_ref[rows, :]

    def z_copy(buf, sem, l, c, where):
        return pltpu.make_async_remote_copy(
            src_ref=buf.at[l, coef, where],
            dst_ref=buf.at[l, coef, where],
            send_sem=sem.at[l, 0, c],
            recv_sem=sem.at[l, 1, c],
            device_id={"coef": other},
            device_id_type=MESH,
        )

    def mixed(buf, l, t):
        own = buf[l, coef, t].astype(jnp.float32)
        return own + dot(d_own[:, :half], buf[l, 0, t]) + dot(d_own[:, half:], buf[l, 1, t])

    def x_copy(l, c, k):
        return pltpu.make_async_remote_copy(
            src_ref=x_buf.at[l, limb, c],
            dst_ref=x_buf.at[l, limb, c],
            send_sem=x_send.at[l, c, k - 1],
            recv_sem=x_recv.at[l, c, k - 1],
            device_id={"limb": lax.rem(limb + k, nl)},
            device_id_type=MESH,
        )

    def x2_copy(l, i, k):
        return pltpu.make_async_remote_copy(
            src_ref=x2_buf.at[l, limb, pl.ds(i * ls, ls)],
            dst_ref=x2_buf.at[l, limb, pl.ds(i * ls, ls)],
            send_sem=x2_send.at[l, i, k - 1],
            recv_sem=x2_recv.at[l, i, k - 1],
            device_id={"limb": lax.rem(limb + k, nl)},
            device_id_type=MESH,
        )

    def switched(l, t_global, t_twist, key_of):
        w = twist[t_twist]
        turned = []
        for d in range(digits):
            total = None
            for s in range(CHUNK):
                at = d * CHUNK + s
                term = x_buf[l, at // lm, at % lm].astype(jnp.float32)
                term = term * up_smem[s, d, t_global]
                total = term if total is None else total + term
            turned.append((total * w).astype(jnp.bfloat16))
        hats = dot(jnp.concatenate(turned, axis=0), c1t)
        sums = [None, None]
        for d in range(digits):
            hat = hats[d * half : (d + 1) * half]
            for i in range(2):
                add = hat * key_of(d, i).astype(jnp.float32)
                sums[i] = add if sums[i] is None else sums[i] + add
        return sums

    def corrected(l, i, q):
        total = None
        for p in range(lp):
            term = x2_buf[l, p // ls, i * ls + p % ls].astype(jnp.float32) * down_smem[p, q]
            total = term if total is None else total + term
        hat = dot((total * twist[q]).astype(jnp.bfloat16), c1t)
        return (s_main[i, q] - hat) * inv_ref[q]

    def put(buf, where, value):
        buf[where] = value

    def finish_b(l, use):
        way_b = ways[l][1]

        for k in range(1, nl):
            x2_copy(l, 0, k).wait_recv()

        def b_part(c, carry):
            for t in range(width):
                b_add[c * width + t] = corrected(l, 0, c * width + t)
            return carry

        lax.fori_loop(0, chunks, b_part, 0)
        way_b.arrive(chunks - 1, (parent_ref[l, n - 1], parent_ref[l, 0]))
        for c in range(chunks):
            way_b.settle(c)
            for t in range(c * width, (c + 1) * width):
                way_b.take(
                    parent_ref[l, me],
                    t,
                    lambda held: use(t, (held.astype(jnp.float32) + b_add[t]).astype(jnp.bfloat16)),
                )

    b_gather[0, me] = root_ref[0]
    tables[0].wait()
    tables[1].wait()

    def send_z(l, t, value):
        z_buf[l, coef, t] = (dot(value, c1) * recip[t]).astype(jnp.bfloat16)

    for c in range(chunks):
        for t in range(c * width, (c + 1) * width):
            send_z(0, t, root_ref[1, t])
        z_copy(z_buf, z_sem, 0, c, part(c)).start()
    tables[2].wait()
    tables[3].wait()

    ways = [
        (Route(2 * l, x_gather, l, 1, False), Route(2 * l + 1, b_gather, l, width, False))
        for l in range(levels)
    ]
    final = [Route(2 * levels + i, f_gather, i, width, True) for i in range(2)]

    for l in range(levels):
        parent = parent_ref[l, me]
        needed = (parent_ref[l, n - 1], parent_ref[l, 0])
        way_x, way_b = ways[l]
        for c in range(chunks):
            z_copy(z_buf, z_sem, l, c, part(c)).wait_recv()
            for t in range(c * width, (c + 1) * width):
                x_gather[l, me, t] = mixed(z_buf, l, t).astype(jnp.bfloat16)
                way_x.start(t)
        if l > 0:
            finish_b(l - 1, lambda t, value: put(b_gather, (l, me, t), value))
        for t in range(lm):
            way_x.arrive(t, needed)
            way_x.settle(t)
            way_x.take(parent, t, lambda value: put(x_buf, (l, limb, t), value))
            for k in range(1, nl):
                x_copy(l, t, k).start()
        for c in range(chunks):
            way_b.start(c)
        if l == 0:
            for copy in scalars:
                copy.wait()
        loads[2 * l].wait()
        loads[2 * l + 1].wait()
        for t in range(lm):
            for k in range(1, nl):
                x_copy(l, t, k).wait_recv()

        for p in range(ls):
            sums = switched(
                l, lq + limb * ls + p, lm + p, lambda d, i: special_key[l, d, i, p]
            )
            for i in range(2):
                z = dot(sums[i].astype(jnp.bfloat16), c1) * recip[lm + p]
                z2_buf[l, coef, i * ls + p] = z.astype(jnp.bfloat16)
        everything = pl.ds(0, 2 * ls)
        z_copy(z2_buf, z2_sem, l, 0, everything).start()
        z_copy(z2_buf, z2_sem, l, 0, everything).wait_recv()
        for i in (1, 0):
            for e in range(i * ls, (i + 1) * ls):
                x2_buf[l, limb, e] = mixed(z2_buf, l, e).astype(jnp.bfloat16)
            for k in range(1, nl):
                x2_copy(l, i, k).start()

        def main_targets(c, carry):
            for t in range(width):
                at = c * width + t
                sums = switched(l, limb * lm + at, at, lambda d, i: main_key[l, d, i, at])
                s_main[0, at] = sums[0]
                s_main[1, at] = sums[1]
            return carry

        lax.fori_loop(0, chunks, main_targets, 0)
        for c in range(chunks - 1):
            way_b.arrive(c, needed)
        for k in range(1, nl):
            x2_copy(l, 1, k).wait_recv()

        last = l == levels - 1
        for c in range(chunks):
            for t in range(c * width, (c + 1) * width):
                value = corrected(l, 1, t).astype(jnp.bfloat16)
                if last:
                    f_gather[1, me, t] = value
                else:
                    send_z(l + 1, t, value)
            if last:
                final[1].start(c)
            else:
                z_copy(z_buf, z_sem, l + 1, c, part(c)).start()

    finish_b(levels - 1, lambda t, value: put(f_gather, (0, me, t), value))
    for c in range(chunks):
        final[0].start(c)
    def store(i, c):
        def one(slot):
            pltpu.make_async_copy(
                final[i].piece(slot, c),
                out_ref.at[i, slot, part(c)],
                store_sem.at[i, slot, c],
            ).start()

        repeat(0, n, one)

    for i in (1, 0):
        for c in range(chunks):
            final[i].arrive(c)
    for i in (1, 0):
        for c in range(chunks):
            final[i].settle(c)
            store(i, c)
    for i in (1, 0):
        for c in range(chunks):

            def stored(slot):
                pltpu.make_async_copy(
                    final[i].piece(slot, c),
                    out_ref.at[i, slot, part(c)],
                    store_sem.at[i, slot, c],
                ).wait()

            repeat(0, n, stored)

    for l in range(levels):
        for way in ways[l]:
            way.end()
        for c in range(chunks):
            z_copy(z_buf, z_sem, l, c, part(c)).wait_send()
        for t in range(lm):
            for k in range(1, nl):
                x_copy(l, t, k).wait_send()
        z_copy(z2_buf, z2_sem, l, 0, pl.ds(0, 2 * ls)).wait_send()
        for k in range(1, nl):
            x2_copy(l, 0, k).wait_send()
            x2_copy(l, 1, k).wait_send()
    for way in final:
        way.end()


def deliver(n, cap, owner_ref, keys_ref, out_ref, held, load_sem, sem):
    me = lax.axis_index("leaf")

    def seek(j, state):
        count, sources, found = state
        mine = (owner_ref[j] == me).astype(jnp.int32)
        hits = [mine * (count == s).astype(jnp.int32) for s in range(cap)]
        sources = tuple(src + hit * j for src, hit in zip(sources, hits))
        found = tuple(f + hit for f, hit in zip(found, hits))
        return count + mine, sources, found

    zero = jnp.int32(0)
    _, sources, found = lax.fori_loop(0, n, seek, (zero, (zero,) * cap, (zero,) * cap))
    for s in range(cap):
        for i in range(2):

            @pl.when(found[s] > 0)
            def _():
                pltpu.make_async_copy(
                    keys_ref.at[i, sources[s]], held.at[s, i], load_sem.at[s, i]
                ).start()

            @pl.when(found[s] == 0)
            def _():
                held[s, i] = jnp.zeros_like(held[s, i])

    for s in range(cap):
        for i in range(2):

            @pl.when(found[s] > 0)
            def _():
                pltpu.make_async_copy(
                    keys_ref.at[i, sources[s]], held.at[s, i], load_sem.at[s, i]
                ).wait()

            pltpu.make_async_copy(held.at[s, i], out_ref.at[s, i], sem.at[s, i]).start()
    for s in range(cap):
        for i in range(2):
            pltpu.make_async_copy(held.at[s, i], out_ref.at[s, i], sem.at[s, i]).wait()


def per_device(
    n,
    nl,
    nc,
    root_keys,
    switch_main,
    switch_special,
    basis_up,
    basis_down,
    special_inverse,
    parent_table,
    owner_table,
):
    cap = 3
    _, levels, digits, _, lm, half, n1 = switch_main.shape
    ls = switch_special.shape[4]
    lq, lp = lm * nl, ls * nl
    n2 = half * nc
    chunks = lm // CHUNK
    c1 = cosine_table(n1)
    c2 = cosine_table(n2).astype(np.float64)
    gram = (c2 @ c2.T - np.eye(n2)).astype(np.float32).astype(ml_dtypes.bfloat16)
    table = twist_table(lq + lp, n1, n2)
    basis_up = basis_up.transpose(2, 0, 1)
    basis_down = basis_down.T
    cfg = (n, nl, lm, ls, lq, lp, digits, levels, cap, half)
    bf16, f32 = jnp.bfloat16, jnp.float32
    tile = (half, n1)
    smem = pl.BlockSpec(memory_space=pltpu.SMEM)
    vmem = pl.BlockSpec(memory_space=pltpu.VMEM)
    hbm = pl.BlockSpec(memory_space=pl.ANY)
    dma = pltpu.SemaphoreType.DMA
    units = 2 * levels + 2
    keys = pl.pallas_call(
        functools.partial(kernel, cfg),
        out_shape=jax.ShapeDtypeStruct((2, n, lm) + tile, bf16),
        in_specs=[smem, vmem, vmem, smem] + [vmem] * 4 + [hbm] * 4,
        out_specs=hbm,
        scratch_shapes=[
            pltpu.VMEM((levels, digits, 2, lm) + tile, bf16),
            pltpu.VMEM((levels, digits, 2, ls) + tile, bf16),
            pltpu.VMEM((lm + ls,) + tile, f32),
            pltpu.VMEM((lm + ls,) + tile, f32),
            pltpu.VMEM((levels, 2, lm) + tile, bf16),
            pltpu.VMEM((levels, n, lm) + tile, bf16),
            pltpu.VMEM((levels, n, lm) + tile, bf16),
            pltpu.VMEM((2, n, lm) + tile, bf16),
            pltpu.VMEM((levels, nl, lm) + tile, bf16),
            pltpu.VMEM((levels, 2, 2 * ls) + tile, bf16),
            pltpu.VMEM((levels, nl, 2 * ls) + tile, bf16),
            pltpu.VMEM((2, lm) + tile, f32),
            pltpu.VMEM((2, ls) + tile, f32),
            pltpu.VMEM((lm,) + tile, f32),
            pltpu.VMEM((2 * levels, 2, lm) + tile, bf16),
            pltpu.VMEM(basis_up.shape, f32),
            pltpu.VMEM(basis_down.shape, f32),
            pltpu.SMEM(basis_up.shape, f32),
            pltpu.SMEM(basis_down.shape, f32),
            dma((2 * levels + 6,)),
            dma((2, n, chunks)),
            dma((units, n, lm)),
            dma((units, 2, n, lm)),
            dma((units, n, lm)),
            dma((levels, 2, chunks)),
            dma((levels, lm, nl - 1)),
            dma((levels, lm, nl - 1)),
            dma((levels, 2, 1)),
            dma((levels, 2, nl - 1)),
            dma((levels, 2, nl - 1)),
        ],
        compiler_params=pltpu.CompilerParams(
            collective_id=0, has_side_effects=True, vmem_limit_bytes=56 * 1024 * 1024
        ),
        name="derive_and_deliver",
    )(
        parent_table,
        basis_up,
        basis_down,
        special_inverse,
        jnp.asarray(c1),
        jnp.asarray(np.ascontiguousarray(c1.T)),
        jnp.asarray(gram),
        root_keys.reshape((2, lm) + tile),
        switch_main,
        switch_special,
        jnp.asarray(table.astype(np.float32)),
        jnp.asarray((1.0 / table).astype(np.float32)),
    )
    out = pl.pallas_call(
        functools.partial(deliver, n, cap),
        out_shape=jax.ShapeDtypeStruct((cap, 2, lm) + tile, bf16),
        in_specs=[smem, hbm],
        out_specs=hbm,
        scratch_shapes=[pltpu.VMEM((cap, 2, lm) + tile, bf16), dma((cap, 2)), dma((cap, 2))],
        compiler_params=pltpu.CompilerParams(vmem_limit_bytes=56 * 1024 * 1024),
        name="deliver",
    )(owner_table, keys)
    return out.reshape((1, cap, 1, 2, lm) + tile)


def solution(mesh):
    sizes = [mesh.shape[axis] for axis in ("leaf", "limb", "coef")]
    return jax.shard_map(
        functools.partial(per_device, *sizes),
        mesh=mesh,
        in_specs=(
            P(("grp", "leaf"), None, None, "limb", "coef", None),
            P(("grp", "leaf"), None, None, None, "limb", "coef", None),
            P(("grp", "leaf"), None, None, None, "limb", "coef", None),
            P(),
            P("limb", None),
            P("limb"),
            P(None, "grp"),
            P("grp"),
        ),
        out_specs=P(("grp", "leaf"), None, None, None, "limb", "coef", None),
        check_vma=False,
    )
```

```python
import functools
import math

import jax
import jax.numpy as jnp
import ml_dtypes
import numpy as np
from jax import lax
from jax.experimental import pallas as pl
from jax.experimental.pallas import tpu as pltpu
from jax.sharding import PartitionSpec as P

MESH = pl.DeviceIdType.MESH
CHUNK = 3


def cosine_table(length):
    frequency = np.arange(length).astype(np.float32)[:, None]
    sample = np.arange(length).astype(np.float32)[None, :]
    weight = np.where(
        frequency == 0, np.sqrt(np.float32(1.0 / length)), np.sqrt(np.float32(2.0 / length))
    )
    angle = np.float32(math.pi) * (np.float32(2.0) * sample + np.float32(1.0)) * frequency
    angle = angle / np.float32(2.0 * length)
    return (weight * np.cos(angle)).astype(ml_dtypes.bfloat16)


def twist_table(limbs, n1, n2):
    product = (
        (2 * np.arange(limbs) + 1)[:, None, None]
        * np.arange(n2)[None, :, None]
        * np.arange(n1)[None, None, :]
        % n2
    )
    return 1.0 + 0.5 * np.cos(2.0 * math.pi * product / n2)


def dot(a, b):
    return jnp.dot(a, b, preferred_element_type=jnp.float32)


def pick(n, index, load):
    if n <= 8:
        value = load(0)
        for j in range(1, n):
            value = jnp.where(index == j, load(j), value)
        return value
    return lax.fori_loop(
        1, n, lambda j, value: jnp.where(index == j, load(j), value), load(0)
    )


def repeat(low, high, body):
    if high - low <= 8:
        for i in range(low, high):
            body(i)
    else:
        lax.fori_loop(low, high, lambda i, c: (body(i), c)[1], 0)


def kernel(
    cfg,
    parent_ref,
    owner_ref,
    up_ref,
    down_ref,
    inv_ref,
    c1_ref,
    c1t_ref,
    d_ref,
    root_ref,
    main_hbm,
    special_hbm,
    twist_hbm,
    recip_hbm,
    out_ref,
    main_key,
    special_key,
    twist,
    recip,
    z_buf,
    x_gather,
    b_gather,
    f_gather,
    x_buf,
    z2_buf,
    x2_buf,
    s_main,
    s_special,
    b_add,
    stage,
    last_stage,
    up_f32,
    down_f32,
    up_smem,
    down_smem,
    load_sem,
    store_sem,
    route_send,
    relay_send,
    route_recv,
    z_sem,
    x_send,
    x_recv,
    z2_sem,
    x2_send,
    x2_recv,
):
    n, nl, lm, ls, lq, lp, digits, levels, cap, half = cfg
    width = CHUNK
    chunks = lm // width
    me = lax.axis_index("leaf")
    limb = lax.axis_index("limb")
    coef = lax.axis_index("coef")
    other = 1 - coef

    loads = []
    for l in range(levels):
        loads.append(pltpu.make_async_copy(main_hbm.at[0, l], main_key.at[l], load_sem.at[l]))
        loads.append(
            pltpu.make_async_copy(special_hbm.at[0, l], special_key.at[l], load_sem.at[levels + l])
        )
    rows = pl.ds(pl.multiple_of(coef * half, half), half)
    tables = []
    for k, (src, dst) in enumerate(((recip_hbm, recip), (twist_hbm, twist))):
        tables.append(
            pltpu.make_async_copy(
                src.at[pl.ds(limb * lm, lm), rows], dst.at[pl.ds(0, lm)], load_sem.at[2 * levels + 2 * k]
            )
        )
        tables.append(
            pltpu.make_async_copy(
                src.at[pl.ds(lq + limb * ls, ls), rows],
                dst.at[pl.ds(lm, ls)],
                load_sem.at[2 * levels + 2 * k + 1],
            )
        )
    up_f32[...] = up_ref[...].astype(jnp.float32)
    down_f32[...] = down_ref[...].astype(jnp.float32)
    scalars = [
        pltpu.make_async_copy(up_f32, up_smem, load_sem.at[2 * levels + 4]),
        pltpu.make_async_copy(down_f32, down_smem, load_sem.at[2 * levels + 5]),
    ]
    for copy in tables + loads + scalars:
        copy.start()

    barrier = pltpu.get_barrier_semaphore()

    def greet(target):
        meets = (target > 0) & (target < n - 1) | (me > 0) & (me < n - 1)

        @pl.when((target != me) & meets)
        def _():
            pl.semaphore_signal(barrier, inc=1, device_id={"leaf": target}, device_id_type=MESH)

    repeat(0, n, greet)
    pl.semaphore_signal(barrier, inc=1, device_id={"coef": other}, device_id_type=MESH)
    for k in range(1, nl):
        pl.semaphore_signal(
            barrier, inc=1, device_id={"limb": lax.rem(limb + k, nl)}, device_id_type=MESH
        )
    at_end = (me == 0) | (me == n - 1)
    pl.semaphore_wait(barrier, nl + jnp.where(at_end, n - 2, n - 1))

    ends = ((n - 2, n - 1, 0), (1, 0, 1))
    inner = (me > 0) & (me < n - 1)

    class Route:
        def __init__(self, unit, buf, lead, width, whole, relays=True):
            self.relays = relays
            self.unit, self.buf, self.lead, self.width, self.whole = unit, buf, lead, width, whole
            self.chunks = lm // width

        def piece(self, slot, c):
            return self.buf.at[self.lead, slot, pl.ds(c * self.width, self.width)]

        def hop(self, slot, c, target):
            return pltpu.make_async_remote_copy(
                src_ref=self.piece(slot, c),
                dst_ref=self.piece(slot, c),
                send_sem=route_send.at[self.unit, target, c],
                recv_sem=route_recv.at[self.unit, slot, c],
                device_id={"leaf": target},
                device_id_type=MESH,
            )

        def relay(self, c, end, side, slot):
            if self.whole and not self.relays:
                source = last_stage.at[slot, pl.ds(c * self.width, self.width)]
            elif self.whole:
                source = self.piece(slot, c)
            else:
                source = stage.at[self.unit, side, pl.ds(c * self.width, self.width)]
            return pltpu.make_async_remote_copy(
                src_ref=source,
                dst_ref=self.piece(slot, c),
                send_sem=relay_send.at[self.unit, side, slot, c],
                recv_sem=route_recv.at[self.unit, slot, c],
                device_id={"leaf": end},
                device_id_type=MESH,
            )

        def start(self, c):
            def one(target):
                @pl.when(target != me)
                def _():
                    self.hop(me, c, target).start()

            if self.whole and self.relays:
                for near, end, side in ends:

                    @pl.when(me == near)
                    def _():
                        self.relay(c, end, side, me).start()

            repeat(1, n - 1, one)

        def arrive(self, c, needed=None):
            @pl.when(inner)
            def _():
                def one(slot):
                    @pl.when(slot != me)
                    def _():
                        self.hop(slot, c, lax.rem(me + 1, n)).wait_recv()
                        if self.whole and self.relays:
                            for near, end, side in ends:

                                @pl.when((me == near) & (slot != end))
                                def _():
                                    self.relay(c, end, side, slot).start()

                repeat(0, n, one)
                if not self.whole and self.relays:
                    for near, end, side in ends:

                        @pl.when(me == near)
                        def _():
                            for t in range(c * self.width, (c + 1) * self.width):
                                stage[self.unit, side, t] = self.choose(needed[side], t)
                            self.relay(c, end, side, me).start()

        def settle(self, c):
            for near, end, side in ends:

                @pl.when(me == end)
                def _():
                    if self.whole:

                        def one(slot):
                            @pl.when(slot != end)
                            def _():
                                self.hop(slot, c, near).wait_recv()

                        repeat(0, n, one)
                    else:
                        self.hop(near, c, near).wait_recv()

        def choose(self, index, t):
            return pick(n, index, lambda j: self.buf[self.lead, j, t])

        def take(self, index, t, use):
            @pl.when(inner)
            def _():
                use(self.choose(index, t))

            for near, end, side in ends:

                @pl.when(me == end)
                def _():
                    own = self.buf[self.lead, end, t]
                    use(jnp.where(index == end, own, self.buf[self.lead, near, t]))

        def sent(self, c):
            def one(target):
                @pl.when(target != me)
                def _():
                    self.hop(me, c, target).wait_send()

            repeat(1, n - 1, one)

        def end(self):
            for c in range(self.chunks):
                if self.relays or not self.whole:
                    self.sent(c)
                else:
                    pl.when(inner)(lambda: self.sent(c))
                for near, end, side in ends:

                    @pl.when(me == near)
                    def _():
                        if self.whole:

                            def other_slot(slot):
                                @pl.when(slot != end)
                                def _():
                                    self.relay(c, end, side, slot).wait_send()

                            repeat(0, n, other_slot)
                        elif self.relays:
                            self.relay(c, end, side, me).wait_send()

    def part(c):
        return pl.ds(c * width, width)

    c1 = c1_ref[...]
    c1t = c1t_ref[...]
    d_own = d_ref[rows, :]

    def z_copy(buf, sem, l, c, where):
        return pltpu.make_async_remote_copy(
            src_ref=buf.at[l, coef, where],
            dst_ref=buf.at[l, coef, where],
            send_sem=sem.at[l, 0, c],
            recv_sem=sem.at[l, 1, c],
            device_id={"coef": other},
            device_id_type=MESH,
        )

    def mixed(buf, l, t):
        own = buf[l, coef, t].astype(jnp.float32)
        return own + dot(d_own[:, :half], buf[l, 0, t]) + dot(d_own[:, half:], buf[l, 1, t])

    def x_copy(l, c, k):
        return pltpu.make_async_remote_copy(
            src_ref=x_buf.at[l, limb, c],
            dst_ref=x_buf.at[l, limb, c],
            send_sem=x_send.at[l, c, k - 1],
            recv_sem=x_recv.at[l, c, k - 1],
            device_id={"limb": lax.rem(limb + k, nl)},
            device_id_type=MESH,
        )

    def x2_copy(l, i, k):
        return pltpu.make_async_remote_copy(
            src_ref=x2_buf.at[l, limb, pl.ds(i * ls, ls)],
            dst_ref=x2_buf.at[l, limb, pl.ds(i * ls, ls)],
            send_sem=x2_send.at[l, i, k - 1],
            recv_sem=x2_recv.at[l, i, k - 1],
            device_id={"limb": lax.rem(limb + k, nl)},
            device_id_type=MESH,
        )

    def switched(l, t_global, t_twist, key_of):
        w = twist[t_twist]
        turned = []
        for d in range(digits):
            total = None
            for s in range(CHUNK):
                at = d * CHUNK + s
                term = x_buf[l, at // lm, at % lm].astype(jnp.float32)
                term = term * up_smem[s, d, t_global]
                total = term if total is None else total + term
            turned.append((total * w).astype(jnp.bfloat16))
        hats = dot(jnp.concatenate(turned, axis=0), c1t)
        sums = [None, None]
        for d in range(digits):
            hat = hats[d * half : (d + 1) * half]
            for i in range(2):
                add = hat * key_of(d, i).astype(jnp.float32)
                sums[i] = add if sums[i] is None else sums[i] + add
        return sums

    def corrected(l, i, q):
        total = None
        for p in range(lp):
            term = x2_buf[l, p // ls, i * ls + p % ls].astype(jnp.float32) * down_smem[p, q]
            total = term if total is None else total + term
        hat = dot((total * twist[q]).astype(jnp.bfloat16), c1t)
        return (s_main[i, q] - hat) * inv_ref[q]

    def put(buf, where, value):
        buf[where] = value

    def finish_b(l, use):
        way_b = ways[l][1]

        for k in range(1, nl):
            x2_copy(l, 0, k).wait_recv()

        def b_part(c, carry):
            for t in range(width):
                b_add[c * width + t] = corrected(l, 0, c * width + t)
            return carry

        lax.fori_loop(0, chunks, b_part, 0)
        way_b.arrive(chunks - 1, (parent_ref[l, n - 1], parent_ref[l, 0]))
        for c in range(chunks):
            if way_b.relays:
                way_b.settle(c)
            for t in range(c * width, (c + 1) * width):

                def total(held):
                    use(t, (held.astype(jnp.float32) + b_add[t]).astype(jnp.bfloat16))

                if way_b.relays:
                    way_b.take(parent_ref[l, me], t, total)
                else:
                    pl.when(inner)(lambda: total(way_b.choose(parent_ref[l, me], t)))
                    pl.when(jnp.logical_not(inner))(
                        lambda: use(t, b_add[t].astype(jnp.bfloat16))
                    )

    def last_b(c):
        last = final[0]
        chunk = range(c * width, (c + 1) * width)
        last.arrive(c)

        @pl.when(inner)
        def _():
            for near, end, side in ends:
                for t in chunk:
                    held = ways[levels - 1][1].choose(parent_ref[levels - 1, end], t)
                    value = f_gather[0, end, t].astype(jnp.float32) + held.astype(jnp.float32)
                    f_gather[0, end, t] = value.astype(jnp.bfloat16)

        for near, end, side in ends:
            spare = jnp.int32(0)
            for k in reversed(range(n)):
                if k != end:
                    spare = jnp.where(owner_ref[k] != end, k, spare)
            swapped = jnp.where(owner_ref[end] == end, spare, n)

            @pl.when(me == near)
            def _():
                def one(slot):
                    @pl.when(slot != end)
                    def _():
                        for t in chunk:
                            last_stage[slot, t] = jnp.where(
                                swapped == slot, f_gather[0, end, t], f_gather[0, slot, t]
                            )
                        last.relay(c, end, side, slot).start()

                repeat(0, n, one)

            @pl.when(me == end)
            def _():
                last.settle(c)
                last.sent(c)
                for t in chunk:
                    f_gather[0, end, t] = pick(n, spare, lambda j: f_gather[0, j, t])

    b_gather[0, me] = root_ref[0]
    tables[0].wait()
    tables[1].wait()

    def send_z(l, t, value):
        z_buf[l, coef, t] = (dot(value, c1) * recip[t]).astype(jnp.bfloat16)

    for c in range(chunks):
        for t in range(c * width, (c + 1) * width):
            send_z(0, t, root_ref[1, t])
        z_copy(z_buf, z_sem, 0, c, part(c)).start()
    tables[2].wait()
    tables[3].wait()

    ways = [
        (
            Route(2 * l, x_gather, l, 1, False),
            Route(2 * l + 1, b_gather, l, width, False, l < levels - 1),
        )
        for l in range(levels)
    ]
    final = [Route(2 * levels + i, f_gather, i, width, True, i == 1) for i in range(2)]

    for l in range(levels):
        parent = parent_ref[l, me]
        needed = (parent_ref[l, n - 1], parent_ref[l, 0])
        way_x, way_b = ways[l]
        for c in range(chunks):
            z_copy(z_buf, z_sem, l, c, part(c)).wait_recv()
            for t in range(c * width, (c + 1) * width):
                x_gather[l, me, t] = mixed(z_buf, l, t).astype(jnp.bfloat16)
                way_x.start(t)
        if l > 0:
            finish_b(l - 1, lambda t, value: put(b_gather, (l, me, t), value))
        for t in range(lm):
            way_x.arrive(t, needed)
            way_x.settle(t)
            way_x.take(parent, t, lambda value: put(x_buf, (l, limb, t), value))
            for k in range(1, nl):
                x_copy(l, t, k).start()
        for c in range(chunks):
            way_b.start(c)
        if l == 0:
            for copy in scalars:
                copy.wait()
        loads[2 * l].wait()
        loads[2 * l + 1].wait()
        for t in range(lm):
            for k in range(1, nl):
                x_copy(l, t, k).wait_recv()

        for p in range(ls):
            sums = switched(
                l, lq + limb * ls + p, lm + p, lambda d, i: special_key[l, d, i, p]
            )
            for i in range(2):
                z = dot(sums[i].astype(jnp.bfloat16), c1) * recip[lm + p]
                z2_buf[l, coef, i * ls + p] = z.astype(jnp.bfloat16)
        everything = pl.ds(0, 2 * ls)
        z_copy(z2_buf, z2_sem, l, 0, everything).start()
        z_copy(z2_buf, z2_sem, l, 0, everything).wait_recv()
        for i in (1, 0):
            for e in range(i * ls, (i + 1) * ls):
                x2_buf[l, limb, e] = mixed(z2_buf, l, e).astype(jnp.bfloat16)
            for k in range(1, nl):
                x2_copy(l, i, k).start()

        def main_targets(c, carry):
            for t in range(width):
                at = c * width + t
                sums = switched(l, limb * lm + at, at, lambda d, i: main_key[l, d, i, at])
                s_main[0, at] = sums[0]
                s_main[1, at] = sums[1]
            return carry

        lax.fori_loop(0, chunks, main_targets, 0)
        for c in range(chunks - 1):
            way_b.arrive(c, needed)
        for k in range(1, nl):
            x2_copy(l, 1, k).wait_recv()

        last = l == levels - 1
        for c in range(chunks):
            for t in range(c * width, (c + 1) * width):
                value = corrected(l, 1, t).astype(jnp.bfloat16)
                if last:
                    f_gather[1, me, t] = value
                else:
                    send_z(l + 1, t, value)
            if last:
                final[1].start(c)
            else:
                z_copy(z_buf, z_sem, l + 1, c, part(c)).start()

    finish_b(levels - 1, lambda t, value: put(f_gather, (0, me, t), value))
    for c in range(chunks):
        final[0].start(c)
    def store(i, c):
        def one(slot):
            pltpu.make_async_copy(
                final[i].piece(slot, c),
                out_ref.at[i, slot, part(c)],
                store_sem.at[i, slot, c],
            ).start()

        repeat(0, n, one)

    for c in range(chunks):
        final[1].arrive(c)
    for c in range(chunks):
        final[1].settle(c)
        store(1, c)
    for c in range(chunks):
        last_b(c)
        store(0, c)
    for i in (1, 0):
        for c in range(chunks):

            def stored(slot):
                pltpu.make_async_copy(
                    final[i].piece(slot, c),
                    out_ref.at[i, slot, part(c)],
                    store_sem.at[i, slot, c],
                ).wait()

            repeat(0, n, stored)

    for l in range(levels):
        for way in ways[l]:
            way.end()
        for c in range(chunks):
            z_copy(z_buf, z_sem, l, c, part(c)).wait_send()
        for t in range(lm):
            for k in range(1, nl):
                x_copy(l, t, k).wait_send()
        z_copy(z2_buf, z2_sem, l, 0, pl.ds(0, 2 * ls)).wait_send()
        for k in range(1, nl):
            x2_copy(l, 0, k).wait_send()
            x2_copy(l, 1, k).wait_send()
    for way in final:
        way.end()


def deliver(n, cap, owner_ref, keys_ref, out_ref, held, load_sem, sem):
    me = lax.axis_index("leaf")

    def seek(j, state):
        count, sources, found = state
        mine = (owner_ref[j] == me).astype(jnp.int32)
        hits = [mine * (count == s).astype(jnp.int32) for s in range(cap)]
        sources = tuple(src + hit * j for src, hit in zip(sources, hits))
        found = tuple(f + hit for f, hit in zip(found, hits))
        return count + mine, sources, found

    zero = jnp.int32(0)
    _, sources, found = lax.fori_loop(0, n, seek, (zero, (zero,) * cap, (zero,) * cap))
    for s in range(cap):
        for i in range(2):

            @pl.when(found[s] > 0)
            def _():
                pltpu.make_async_copy(
                    keys_ref.at[i, sources[s]], held.at[s, i], load_sem.at[s, i]
                ).start()

            @pl.when(found[s] == 0)
            def _():
                held[s, i] = jnp.zeros_like(held[s, i])

    for s in range(cap):
        for i in range(2):

            @pl.when(found[s] > 0)
            def _():
                pltpu.make_async_copy(
                    keys_ref.at[i, sources[s]], held.at[s, i], load_sem.at[s, i]
                ).wait()

            pltpu.make_async_copy(held.at[s, i], out_ref.at[s, i], sem.at[s, i]).start()
    for s in range(cap):
        for i in range(2):
            pltpu.make_async_copy(held.at[s, i], out_ref.at[s, i], sem.at[s, i]).wait()


def per_device(
    n,
    nl,
    nc,
    root_keys,
    switch_main,
    switch_special,
    basis_up,
    basis_down,
    special_inverse,
    parent_table,
    owner_table,
):
    cap = 3
    _, levels, digits, _, lm, half, n1 = switch_main.shape
    ls = switch_special.shape[4]
    lq, lp = lm * nl, ls * nl
    n2 = half * nc
    chunks = lm // CHUNK
    c1 = cosine_table(n1)
    c2 = cosine_table(n2).astype(np.float64)
    gram = (c2 @ c2.T - np.eye(n2)).astype(np.float32).astype(ml_dtypes.bfloat16)
    table = twist_table(lq + lp, n1, n2)
    basis_up = basis_up.transpose(2, 0, 1)
    basis_down = basis_down.T
    cfg = (n, nl, lm, ls, lq, lp, digits, levels, cap, half)
    bf16, f32 = jnp.bfloat16, jnp.float32
    tile = (half, n1)
    smem = pl.BlockSpec(memory_space=pltpu.SMEM)
    vmem = pl.BlockSpec(memory_space=pltpu.VMEM)
    hbm = pl.BlockSpec(memory_space=pl.ANY)
    dma = pltpu.SemaphoreType.DMA
    units = 2 * levels + 2
    keys = pl.pallas_call(
        functools.partial(kernel, cfg),
        out_shape=jax.ShapeDtypeStruct((2, n, lm) + tile, bf16),
        in_specs=[smem, smem, vmem, vmem, smem] + [vmem] * 4 + [hbm] * 4,
        out_specs=hbm,
        scratch_shapes=[
            pltpu.VMEM((levels, digits, 2, lm) + tile, bf16),
            pltpu.VMEM((levels, digits, 2, ls) + tile, bf16),
            pltpu.VMEM((lm + ls,) + tile, f32),
            pltpu.VMEM((lm + ls,) + tile, f32),
            pltpu.VMEM((levels, 2, lm) + tile, bf16),
            pltpu.VMEM((levels, n, lm) + tile, bf16),
            pltpu.VMEM((levels, n, lm) + tile, bf16),
            pltpu.VMEM((2, n, lm) + tile, bf16),
            pltpu.VMEM((levels, nl, lm) + tile, bf16),
            pltpu.VMEM((levels, 2, 2 * ls) + tile, bf16),
            pltpu.VMEM((levels, nl, 2 * ls) + tile, bf16),
            pltpu.VMEM((2, lm) + tile, f32),
            pltpu.VMEM((2, ls) + tile, f32),
            pltpu.VMEM((lm,) + tile, f32),
            pltpu.VMEM((2 * levels, 2, lm) + tile, bf16),
            pltpu.VMEM((n, lm) + tile, bf16),
            pltpu.VMEM(basis_up.shape, f32),
            pltpu.VMEM(basis_down.shape, f32),
            pltpu.SMEM(basis_up.shape, f32),
            pltpu.SMEM(basis_down.shape, f32),
            dma((2 * levels + 6,)),
            dma((2, n, chunks)),
            dma((units, n, lm)),
            dma((units, 2, n, lm)),
            dma((units, n, lm)),
            dma((levels, 2, chunks)),
            dma((levels, lm, nl - 1)),
            dma((levels, lm, nl - 1)),
            dma((levels, 2, 1)),
            dma((levels, 2, nl - 1)),
            dma((levels, 2, nl - 1)),
        ],
        compiler_params=pltpu.CompilerParams(
            collective_id=0, has_side_effects=True, vmem_limit_bytes=56 * 1024 * 1024
        ),
        name="derive_and_deliver",
    )(
        parent_table,
        owner_table,
        basis_up,
        basis_down,
        special_inverse,
        jnp.asarray(c1),
        jnp.asarray(np.ascontiguousarray(c1.T)),
        jnp.asarray(gram),
        root_keys.reshape((2, lm) + tile),
        switch_main,
        switch_special,
        jnp.asarray(table.astype(np.float32)),
        jnp.asarray((1.0 / table).astype(np.float32)),
    )
    out = pl.pallas_call(
        functools.partial(deliver, n, cap),
        out_shape=jax.ShapeDtypeStruct((cap, 2, lm) + tile, bf16),
        in_specs=[smem, hbm],
        out_specs=hbm,
        scratch_shapes=[pltpu.VMEM((cap, 2, lm) + tile, bf16), dma((cap, 2)), dma((cap, 2))],
        compiler_params=pltpu.CompilerParams(vmem_limit_bytes=56 * 1024 * 1024),
        name="deliver",
    )(owner_table, keys)
    return out.reshape((1, cap, 1, 2, lm) + tile)


def solution(mesh):
    sizes = [mesh.shape[axis] for axis in ("leaf", "limb", "coef")]
    return jax.shard_map(
        functools.partial(per_device, *sizes),
        mesh=mesh,
        in_specs=(
            P(("grp", "leaf"), None, None, "limb", "coef", None),
            P(("grp", "leaf"), None, None, None, "limb", "coef", None),
            P(("grp", "leaf"), None, None, None, "limb", "coef", None),
            P(),
            P("limb", None),
            P("limb"),
            P(None, "grp"),
            P("grp"),
        ),
        out_specs=P(("grp", "leaf"), None, None, None, "limb", "coef", None),
        check_vma=False,
    )
```
